128 devices in a mesh: gx: 8 (over y, core), gy: 16 (over z, x).
Axes of the slice: x: 4, y: 4, z: 4, core: 2. Of those that a mesh axis runs over, the one named last changes fastest.
Arguments:
- fields: float32 [5, 8, 2048, 2048], P(None, None, 'gx', 'gy'), may hold values from -8 to 8
Outputs:
- x_derivative: float32 [5, 8, 2048, 2048], P(None, None, 'gx', 'gy')
- y_derivative: float32 [5, 8, 2048, 2048], P(None, None, 'gx', 'gy')
- smoothed: float32 [5, 8, 2048, 2048], P(None, None, 'gx', 'gy')
The draws below stay inside these ranges and needn't reach their ends.
All inputs are finite; a program needn't handle non-finite values.
Results may differ from the reference program's by a relative error of at most 0.0003.
Values sent between devices are 32-bit elements; how exact they have to be, the bound alone decides.
No kernel may reach another device: no remote copies, remote signals or barrier semaphores. Data moves between devices by JAX's collectives and lax.ppermute only.
A program may use at most 192 MiB of HBM per device.

```python
import math
import jax
import jax.numpy as jnp
from jax import lax

FIELDS = 5
NZ = 8
NX = 2048
NY = 2048


def draw_fields(key, part):
    key = jax.random.fold_in(key, 11)
    rough_key = jax.random.fold_in(key, 0)
    sign_key = jax.random.fold_in(key, 2)
    signs = (jax.random.randint(sign_key, (2, FIELDS, NZ, 1, 1), 0, 2) * 2 - 1).astype(jnp.float32)
    row_pattern = (1 - 2 * (jnp.arange(NX) % 2)).astype(jnp.float32)[:, None]
    column_pattern = (1 - 2 * (jnp.arange(NY) % 2)).astype(jnp.float32)[None, :]
    alternating = 3.0 * (signs[0] * row_pattern + signs[1] * column_pattern)
    rough = jnp.clip(0.5 * jax.random.normal(rough_key, (FIELDS, NZ, NX, NY), jnp.float32), -2.0, 2.0)
    return rough + alternating


def setup_inputs(seed: int = 0) -> dict:
    splits = jax.random.split(jax.random.key(seed), 2)
    return {
        "fields": draw_fields(jax.random.fold_in(splits[1], 71), 0),
    }


alpha_deriv = 1.0 / 3.0
coef_near = 14.0 / 9.0
coef_far = 1.0 / 9.0
alpha_filter = 0.45


def filter_weights():
    alpha = alpha_filter
    return [(193.0 + 126.0 * alpha) / 256.0, (105.0 + 302.0 * alpha) / 256.0,
            15.0 * (2.0 * alpha - 1.0) / 64.0, 45.0 * (1.0 - 2.0 * alpha) / 512.0,
            5.0 * (2.0 * alpha - 1.0) / 256.0, (1.0 - 2.0 * alpha) / 512.0]


def spectral(one_field, axis_dim, cells, derivative):
    wavenumbers = jnp.arange(cells // 2 + 1).astype(one_field.dtype) * (2.0 * math.pi / cells)
    if derivative:
        numerator = coef_near * jnp.sin(wavenumbers) + 0.5 * coef_far * jnp.sin(2.0 * wavenumbers)
        response = numerator / (1.0 + 2.0 * alpha_deriv * jnp.cos(wavenumbers))
    else:
        weights = filter_weights()
        numerator = weights[0] + jnp.zeros_like(wavenumbers)
        for order in range(1, 6):
            numerator = numerator + weights[order] * jnp.cos(order * wavenumbers)
        response = numerator / (1.0 + 2.0 * alpha_filter * jnp.cos(wavenumbers))
    arrangement = [1, 1, 1]
    arrangement[axis_dim] = cells // 2 + 1
    response = response.reshape(arrangement)
    spectrum = jnp.fft.rfft(one_field, axis=axis_dim)
    if derivative:
        spectrum = spectrum * (1j * response)
    else:
        spectrum = spectrum * response
    return jnp.fft.irfft(spectrum, n=cells, axis=axis_dim).astype(one_field.dtype)


def reference(fields):
    def per_field(one_field):
        along_x = spectral(one_field, 1, NX, True)
        along_y = spectral(one_field, 2, NY, True)
        x_filtered = spectral(one_field, 1, NX, False)
        smoothed = spectral(x_filtered, 2, NY, False)
        return along_x, along_y, smoothed

    x_derivative, y_derivative, smoothed = lax.map(per_field, fields)
    return x_derivative, y_derivative, smoothed
```

```python
import math

import jax
import jax.numpy as jnp
import ml_dtypes
import numpy as np
from jax import lax
from jax.experimental import pallas as pl
from jax.experimental.pallas import tpu as pltpu
from jax.sharding import PartitionSpec as P

F32 = jnp.float32
BF16 = jnp.bfloat16
deriv_offdiag = 1.0 / 3.0
coef_near = 14.0 / 9.0
coef_far = 1.0 / 9.0
filter_offdiag = 0.45
reach = 64
filter_rim = 48
deriv_rim = 24
group = 8


def filter_weights():
    return [
        (193.0 + 126.0 * filter_offdiag) / 256.0,
        (105.0 + 302.0 * filter_offdiag) / 256.0,
        15.0 * (2.0 * filter_offdiag - 1.0) / 64.0,
        45.0 * (1.0 - 2.0 * filter_offdiag) / 512.0,
        5.0 * (2.0 * filter_offdiag - 1.0) / 256.0,
        (1.0 - 2.0 * filter_offdiag) / 512.0,
    ]


class Line:
    def __init__(self, offdiag, taps, sign, width):
        gap = math.sqrt(1.0 - 4.0 * offdiag * offdiag)
        self.ratio = (gap - 1.0) / (2.0 * offdiag)
        self.gap = gap
        self.taps = taps
        self.sign = sign
        far = width + 4
        self.scale = self.tap(far) / self.ratio**far
        self.near = [0.0] + [
            self.tap(n) - self.scale * self.ratio**n if n <= width else 0.0 for n in range(1, 2 * far)
        ]

    def tap(self, n):
        return sum(w * self.ratio ** abs(n - o) / self.gap for o, w in self.taps)

    def block(self, cells):
        values = np.array([self.tap(n) for n in range(-cells + 1, cells)])
        ids = np.arange(cells)
        return values[ids[None, :] - ids[:, None] + cells - 1]

    def near_at(self, n):
        return self.near[n] if 0 < n < len(self.near) else 0.0

    def from_below(self, cells):
        table = np.zeros((cells, 5))
        for i in range(cells):
            table[i, 0] = self.sign * self.scale * self.ratio ** (i + 1)
            for k in range(4):
                table[i, 1 + k] = self.sign * self.near_at(i + 4 - k)
        return table

    def from_above(self, cells):
        table = np.zeros((cells, 5))
        for i in range(cells):
            table[i, 0] = self.scale * self.ratio ** (cells - i)
            for k in range(4):
                table[i, 1 + k] = self.near_at(cells + k - i)
        return table


def line_operators():
    weights = filter_weights()
    deriv_taps = [
        (-2, -coef_far / 4.0),
        (-1, -coef_near / 2.0),
        (1, coef_near / 2.0),
        (2, coef_far / 4.0),
    ]
    filter_taps = [(0, weights[0])]
    for order in range(1, 6):
        filter_taps.append((order, weights[order] / 2.0))
        filter_taps.append((-order, weights[order] / 2.0))
    return Line(deriv_offdiag, deriv_taps, -1.0, 1), Line(filter_offdiag, filter_taps, 1.0, 4)


def halves(table):
    hi = np.asarray(table, np.float32).astype(ml_dtypes.bfloat16)
    lo = (np.asarray(table, np.float64) - hi.astype(np.float64)).astype(ml_dtypes.bfloat16)
    return hi, lo


def split(values):
    hi = values.astype(BF16)
    return hi, (values - hi.astype(F32)).astype(BF16)


def dot(a, b, dims=((1,), (0,))):
    return lax.dot_general(a, b, (dims, ((), ())), preferred_element_type=F32)


def lanes(column):
    return np.repeat(np.asarray(column, np.float32)[:, None], 128, axis=1)


VMEM = pl.BlockSpec(memory_space=pltpu.VMEM)
ANY = pl.BlockSpec(memory_space=pl.ANY)


def call(name, kernel, outs, ins, flops, nbytes, out_specs=None, scratch=(), limit=20):
    return pl.pallas_call(
        kernel,
        in_specs=[VMEM] * len(ins),
        out_specs=out_specs or [VMEM] * len(outs),
        out_shape=[jax.ShapeDtypeStruct(shape, F32) for shape in outs],
        scratch_shapes=list(scratch),
        compiler_params=pltpu.CompilerParams(vmem_limit_bytes=limit << 20),
        cost_estimate=pl.CostEstimate(flops=flops, bytes_accessed=nbytes, transcendentals=0),
        name=name,
    )(*ins)


def face_kernel(f, wf_head, wd_head, wf_tail, wd_tail, ty, x_down, x_up, y_down, y_up):
    planes, rows, _ = f.shape
    short = wd_head.shape[0]

    def step(i, carry):
        for j in range(group):
            p = i * group + j
            head = f[p, :reach, :]
            tail = f[p, rows - reach :, :]
            row = pl.ds(p, 1)
            x_down[0, row, :] = jnp.sum(head * wf_head[...], axis=0, keepdims=True)
            x_up[0, row, :] = jnp.sum(tail * wf_tail[...], axis=0, keepdims=True)
            x_down[5, row, :] = jnp.sum(head[:short] * wd_head[...], axis=0, keepdims=True)
            x_up[5, row, :] = jnp.sum(tail[reach - short :] * wd_tail[...], axis=0, keepdims=True)
            for k in range(4):
                x_down[1 + k, row, :] = f[p, k : k + 1, :]
                x_up[1 + k, row, :] = f[p, rows - 4 + k : rows - 3 + k, :]
            both = jnp.concatenate(split(f[p]), axis=-1)
            r = dot(ty[...], both, ((1,), (1,)))
            r = r[:16] + r[16:]
            for k in range(6):
                y_down[k, row, :] = r[k : k + 1]
                y_up[k, row, :] = r[8 + k : 9 + k]
        return carry

    lax.fori_loop(0, planes // group, step, 0)


def x_product(f, w, i):
    hi, lo = split(jnp.concatenate([f[2 * i], f[2 * i + 1]], axis=-1))
    n = hi.shape[0]
    return dot(w[:, :n], hi) + dot(w[:, n:], hi) + dot(w[:, :n], lo)


def filter_x_kernel(f, w, out):
    planes = f.shape[0]
    pairs = group // 2

    def step(i, carry):
        for j in range(pairs):
            q = i * pairs + j
            r = x_product(f, w, q)
            out[2 * q] = r[:, :128]
            out[2 * q + 1] = r[:, 128:]
        return carry

    lax.fori_loop(0, planes // group, step, 0)


def corner_kernel(lower, upper, ty_hi, ty_lo, out):
    planes = lower.shape[1]
    rows = jnp.concatenate([lower[k] for k in range(5)] + [upper[k] for k in range(5)], axis=0)
    hi, lo = split(rows)
    r = dot(hi, ty_hi[...]) + dot(hi, ty_lo[...]) + dot(lo, ty_hi[...])
    total = r[:planes]
    for k in range(1, 10):
        total = total + pltpu.roll(r[k * planes : (k + 1) * planes], 10 * k, 1)
    out[...] = total


def add_rims(values, low, high):
    n = low.shape[0]
    return jnp.concatenate([values[:n] + low, values[n:-n], values[-n:] + high], axis=0)


def filter_rims(lower, upper, s_low, s_high, c_low, c_high, row):
    low = s_low[...] * lower[0, row, :]
    high = s_high[...] * upper[0, row, :]
    near_low = c_low[0] * lower[1, row, :]
    near_high = c_high[0] * upper[1, row, :]
    for k in range(1, 4):
        near_low = near_low + c_low[k] * lower[1 + k, row, :]
        near_high = near_high + c_high[k] * upper[1 + k, row, :]
    low = jnp.concatenate([low[:8] + near_low, low[8:]], axis=0)
    high = jnp.concatenate([high[:-8], high[-8:] + near_high], axis=0)
    return low, high


def deriv_rims(lower, upper, s_low, s_high, c_low, c_high, row):
    low = s_low[...] * lower[5, row, :]
    high = s_high[...] * upper[5, row, :]
    low = jnp.concatenate([low[:8] + c_low[...] * lower[4, row, :], low[8:]], axis=0)
    high = jnp.concatenate([high[:-8], high[-8:] + c_high[...] * upper[1, row, :]], axis=0)
    return low, high


def middle_kernel(
    f, fx, lower, upper, wx, wy_d, wy_f, fs_low, fs_high, fc_low, fc_high, ds_low, ds_high, dc_low, dc_high,
    dx_out, dy, sm, dx, sems,
):
    planes = f.shape[0]
    pairs = group // 2

    def x_step(i, carry):
        for j in range(pairs):
            q = i * pairs + j
            r = x_product(f, wx, q)
            for half in range(2):
                p = 2 * q + half
                low, high = deriv_rims(lower, upper, ds_low, ds_high, dc_low, dc_high, pl.ds(p, 1))
                dx[p] = add_rims(r[:, 128 * half : 128 * half + 128], low, high)
        part = pl.ds(i * group, group)
        pltpu.make_async_copy(dx.at[part], dx_out.at[part], sems.at[i]).start()
        return carry

    lax.fori_loop(0, planes // group, x_step, 0)

    def y_step(i, carry):
        for j in range(group):
            p = i * group + j
            r = dot(jnp.concatenate(split(f[p]), axis=-1), wy_d[...])
            dy[p] = r[:, :128] + r[:, 128:]
            low, high = filter_rims(lower, upper, fs_low, fs_high, fc_low, fc_high, pl.ds(p, 1))
            r = dot(jnp.concatenate(split(add_rims(fx[p], low, high)), axis=-1), wy_f[...])
            sm[p] = r[:, :128] + r[:, 128:]
        return carry

    lax.fori_loop(0, planes // group, y_step, 0)
    for i in range(planes // group):
        part = pl.ds(i * group, group)
        pltpu.make_async_copy(dx.at[part], dx_out.at[part], sems.at[i]).wait()


def last_kernel(
    dy, sm, lower, upper, z_lower, z_upper, ax, ux, v, dy_out, sm_out, halo, dy_full, sm_full, sems
):
    planes = dy.shape[0]
    n = ax.shape[0]
    rows = jnp.concatenate([lower[k] for k in range(5)] + [upper[k] for k in range(5)], axis=0)
    hi, lo = split(rows)
    filtered = dot(hi, ax[:, :n]) + dot(hi, ax[:, n:]) + dot(lo, ax[:, :n])
    corners = jnp.concatenate(
        [pltpu.roll(z_lower[...], 128 - 5 - g, 1) for g in range(5)]
        + [z_upper[...]]
        + [pltpu.roll(z_upper[...], 128 - g, 1) for g in range(1, 5)],
        axis=0,
    )
    hi, lo = split(corners)
    filtered = filtered + dot(hi, ux[:, :n]) + dot(hi, ux[:, n:]) + dot(lo, ux[:, :n])
    zero = jnp.zeros((planes, n), F32)
    table = [filtered[k * planes : (k + 1) * planes] for k in range(5)] + [lower[5], lower[4], zero]
    table += [filtered[(5 + k) * planes : (6 + k) * planes] for k in range(5)] + [upper[5], upper[1], zero]
    for k in range(16):
        for c in range(0, n, 128):
            halo[c // 128, pl.ds(k, planes, stride=16), :] = table[k][:, c : c + 128]

    def step(i, carry):
        for j in range(group):
            p = i * group + j
            at = pl.ds(pl.multiple_of(p * 16, 16), 16)
            hi, lo = split(jnp.concatenate([halo[c, at, :] for c in range(n // 128)], axis=-1))
            r = dot(jnp.concatenate([hi, lo, hi], axis=0), v[...], ((0,), (0,)))
            dy_full[p] = dy[p] + r[:, :128]
            sm_full[p] = sm[p] + r[:, 128:]
        part = pl.ds(i * group, group)
        pltpu.make_async_copy(dy_full.at[part], dy_out.at[part], sems.at[0, i]).start()
        pltpu.make_async_copy(sm_full.at[part], sm_out.at[part], sems.at[1, i]).start()
        return carry

    lax.fori_loop(0, planes // group, step, 0)
    for i in range(planes // group):
        part = pl.ds(i * group, group)
        pltpu.make_async_copy(dy_full.at[part], dy_out.at[part], sems.at[0, i]).wait()
        pltpu.make_async_copy(sm_full.at[part], sm_out.at[part], sems.at[1, i]).wait()


def tables(rows, cols):
    deriv, smooth = line_operators()
    t = {}
    for name, line in (("d", deriv), ("f", smooth)):
        hi, lo = halves(line.block(rows))
        t["wx_" + name] = np.concatenate([hi, lo], axis=1)
        hi, lo = halves(line.block(cols).T)
        t["wy_" + name] = np.block([[hi, lo], [hi, np.zeros_like(lo)]])
    hi, lo = halves(smooth.block(rows).T)
    t["ax"] = np.concatenate([hi, lo], axis=1)
    powers = lambda line, count: line.ratio ** np.arange(count)
    short = 32
    t["wf_head"] = lanes(powers(smooth, reach))
    t["wf_tail"] = lanes(powers(smooth, reach)[::-1])
    t["wd_head"] = lanes(powers(deriv, short))
    t["wd_tail"] = lanes(powers(deriv, short)[::-1])
    ty = np.zeros((16, cols))
    ty[0] = powers(smooth, cols)
    ty[8] = ty[0][::-1]
    for k in range(4):
        ty[1 + k, k] = 1.0
        ty[9 + k, cols - 4 + k] = 1.0
    ty[5] = powers(deriv, cols)
    ty[13] = ty[5][::-1]
    hi, lo = halves(ty)
    t["ty"] = np.block([[hi, hi], [lo, np.zeros_like(lo)]])
    columns = np.zeros((cols, 128))
    columns[:, :5] = ty[:5].T
    columns[:, 5:10] = ty[8:13].T
    t["ty_hi"], t["ty_lo"] = halves(columns)
    low, high = smooth.from_below(rows), smooth.from_above(rows)
    ux = np.zeros((128, rows))
    for k in range(5):
        ux[10 * k] = low[:, k]
        ux[10 * (5 + k)] = high[:, k]
    hi, lo = halves(ux)
    t["ux"] = np.concatenate([hi, lo], axis=1)
    t["fs_low"], t["fs_high"] = lanes(low[:filter_rim, 0]), lanes(high[-filter_rim:, 0])
    t["fc_low"] = np.stack([lanes(low[:8, 1 + k]) for k in range(4)])
    t["fc_high"] = np.stack([lanes(high[-8:, 1 + k]) for k in range(4)])
    low, high = deriv.from_below(rows), deriv.from_above(rows)
    t["ds_low"], t["ds_high"] = lanes(low[:deriv_rim, 0]), lanes(high[-deriv_rim:, 0])
    t["dc_low"], t["dc_high"] = lanes(low[:8, 4]), lanes(high[-8:, 1])
    v = np.zeros((16, 2 * cols))
    low, high = smooth.from_below(cols), smooth.from_above(cols)
    v[0:5, cols:], v[8:13, cols:] = low.T, high.T
    low, high = deriv.from_below(cols), deriv.from_above(cols)
    v[5, :cols], v[6, :cols] = low[:, 0], low[:, 4]
    v[13, :cols], v[14, :cols] = high[:, 0], high[:, 1]
    hi, lo = halves(v)
    t["v"] = np.concatenate([hi, hi, lo], axis=0)
    return {key: jnp.asarray(value) for key, value in t.items()}


def shifted(values, axis, by):
    count = lax.axis_size(axis)
    return lax.ppermute(values, axis, [(i, (i + by) % count) for i in range(count)])


def on_device(fields):
    shape = fields.shape
    rows, cols = shape[2:]
    planes = shape[0] * shape[1]
    block = (planes, rows, cols)
    f = fields.reshape(block)
    t = tables(rows, cols)
    x_face, y_face = (6, planes, cols), (6, planes, rows)
    x_down, x_up, y_down, y_up = call(
        "faces", face_kernel, [x_face, x_face, y_face, y_face],
        [f] + [t[k] for k in ("wf_head", "wd_head", "wf_tail", "wd_tail", "ty")], 10**9, 10**7,
    )
    y_lower = shifted(y_up, "gy", 1)
    y_upper = shifted(y_down, "gy", -1)
    x_lower = shifted(x_up, "gx", 1)
    x_upper = shifted(x_down, "gx", -1)
    (fx,) = call("filter_x", filter_x_kernel, [block], [f, t["wx_f"]], 2 * 10**9, 10**7)
    (corner,) = call(
        "corners", corner_kernel, [(planes, 128)], [x_lower, x_upper, t["ty_hi"], t["ty_lo"]], 10**8, 10**6
    )
    z_lower = shifted(corner, "gy", 1)
    z_upper = shifted(corner, "gy", -1)
    rims = ("fs_low", "fs_high", "fc_low", "fc_high", "ds_low", "ds_high", "dc_low", "dc_high")
    dx, dy, sm = call(
        "middle", middle_kernel, [block, block, block],
        [f, fx, x_lower, x_upper] + [t[k] for k in ("wx_d", "wy_d", "wy_f") + rims], 6 * 10**9, 2 * 10**7,
        out_specs=[ANY, VMEM, VMEM],
        scratch=[pltpu.VMEM(block, F32), pltpu.SemaphoreType.DMA((planes // group,))],
    )
    dy, sm = call(
        "last", last_kernel, [block, block],
        [dy, sm, y_lower, y_upper, z_lower, z_upper, t["ax"], t["ux"], t["v"]], 10**9, 2 * 10**7,
        out_specs=[ANY, ANY],
        scratch=[
            pltpu.VMEM((rows // 128, planes * 16, 128), F32),
            pltpu.VMEM(block, F32),
            pltpu.VMEM(block, F32),
            pltpu.SemaphoreType.DMA((2, planes // group)),
        ],
        limit=24,
    )
    return tuple(out.reshape(shape) for out in (dx, dy, sm))


def solution(mesh):
    placed = P(None, None, "gx", "gy")
    return jax.shard_map(
        on_device, mesh=mesh, in_specs=(placed,), out_specs=(placed, placed, placed), check_vma=False
    )
```

```python
import math

import jax
import jax.numpy as jnp
import ml_dtypes
import numpy as np
from jax import lax
from jax.experimental import pallas as pl
from jax.experimental.pallas import tpu as pltpu
from jax.sharding import PartitionSpec as P

F32 = jnp.float32
BF16 = jnp.bfloat16
deriv_offdiag = 1.0 / 3.0
coef_near = 14.0 / 9.0
coef_far = 1.0 / 9.0
filter_offdiag = 0.45
reach = 64
filter_rim = 48
deriv_rim = 24
group = 8


def filter_weights():
    return [
        (193.0 + 126.0 * filter_offdiag) / 256.0,
        (105.0 + 302.0 * filter_offdiag) / 256.0,
        15.0 * (2.0 * filter_offdiag - 1.0) / 64.0,
        45.0 * (1.0 - 2.0 * filter_offdiag) / 512.0,
        5.0 * (2.0 * filter_offdiag - 1.0) / 256.0,
        (1.0 - 2.0 * filter_offdiag) / 512.0,
    ]


class Line:
    def __init__(self, offdiag, taps, sign, width):
        gap = math.sqrt(1.0 - 4.0 * offdiag * offdiag)
        self.ratio = (gap - 1.0) / (2.0 * offdiag)
        self.gap = gap
        self.taps = taps
        self.sign = sign
        far = width + 4
        self.scale = self.tap(far) / self.ratio**far
        self.near = [0.0] + [
            self.tap(n) - self.scale * self.ratio**n if n <= width else 0.0 for n in range(1, 2 * far)
        ]

    def tap(self, n):
        return sum(w * self.ratio ** abs(n - o) / self.gap for o, w in self.taps)

    def block(self, cells):
        values = np.array([self.tap(n) for n in range(-cells + 1, cells)])
        ids = np.arange(cells)
        return values[ids[None, :] - ids[:, None] + cells - 1]

    def near_at(self, n):
        return self.near[n] if 0 < n < len(self.near) else 0.0

    def from_below(self, cells):
        table = np.zeros((cells, 5))
        for i in range(cells):
            table[i, 0] = self.sign * self.scale * self.ratio ** (i + 1)
            for k in range(4):
                table[i, 1 + k] = self.sign * self.near_at(i + 4 - k)
        return table

    def from_above(self, cells):
        table = np.zeros((cells, 5))
        for i in range(cells):
            table[i, 0] = self.scale * self.ratio ** (cells - i)
            for k in range(4):
                table[i, 1 + k] = self.near_at(cells + k - i)
        return table


def line_operators():
    weights = filter_weights()
    deriv_taps = [
        (-2, -coef_far / 4.0),
        (-1, -coef_near / 2.0),
        (1, coef_near / 2.0),
        (2, coef_far / 4.0),
    ]
    filter_taps = [(0, weights[0])]
    for order in range(1, 6):
        filter_taps.append((order, weights[order] / 2.0))
        filter_taps.append((-order, weights[order] / 2.0))
    return Line(deriv_offdiag, deriv_taps, -1.0, 1), Line(filter_offdiag, filter_taps, 1.0, 4)


def halves(table):
    hi = np.asarray(table, np.float32).astype(ml_dtypes.bfloat16)
    lo = (np.asarray(table, np.float64) - hi.astype(np.float64)).astype(ml_dtypes.bfloat16)
    return hi, lo


def split(values):
    hi = values.astype(BF16)
    return hi, (values - hi.astype(F32)).astype(BF16)


def dot(a, b, dims=((1,), (0,))):
    return lax.dot_general(a, b, (dims, ((), ())), preferred_element_type=F32)


def lanes(column):
    return np.repeat(np.asarray(column, np.float32)[:, None], 128, axis=1)


VMEM = pl.BlockSpec(memory_space=pltpu.VMEM)
ANY = pl.BlockSpec(memory_space=pl.ANY)


def call(name, kernel, outs, ins, flops, nbytes, in_specs=None, out_specs=None, scratch=(), limit=20, aliases=None):
    return pl.pallas_call(
        kernel,
        in_specs=in_specs or [VMEM] * len(ins),
        out_specs=out_specs or [VMEM] * len(outs),
        out_shape=[jax.ShapeDtypeStruct(shape, F32) for shape in outs],
        scratch_shapes=list(scratch),
        input_output_aliases=aliases or {},
        compiler_params=pltpu.CompilerParams(vmem_limit_bytes=limit << 20),
        cost_estimate=pl.CostEstimate(flops=flops, bytes_accessed=nbytes, transcendentals=0),
        name=name,
    )(*ins)


def powers_of(ratio, exponent, bits):
    out = jnp.where(exponent & 1 == 1, F32(ratio), F32(1.0))
    for b in range(1, bits):
        out = out * jnp.where((exponent >> b) & 1 == 1, F32(ratio ** (1 << b)), F32(1.0))
    return out


def y_functionals(cols):
    deriv, smooth = line_operators()
    shape = (8, cols)
    at = lax.broadcasted_iota(jnp.int32, shape, 1)
    row = lax.broadcasted_iota(jnp.int32, shape, 0)
    parts = []
    for place, first in ((at, at - (row - 1)), (cols - 1 - at, at - (cols - 5 + row))):
        cell = jnp.where((first == 0) & (row >= 1) & (row <= 4), F32(1.0), F32(0.0))
        cell = jnp.where(row == 0, powers_of(smooth.ratio, place, 7), cell)
        parts.append(jnp.where(row == 5, powers_of(deriv.ratio, place, 7), cell))
    hi, lo = split(jnp.concatenate(parts, axis=0))
    return jnp.concatenate(
        [jnp.concatenate([hi, hi], axis=1), jnp.concatenate([lo, jnp.zeros_like(lo)], axis=1)], axis=0
    )


def geometric(values, ratio, weights, tail):
    tiles = [values[8 * j : 8 * j + 8] for j in range(values.shape[0] // 8)]
    if not tail:
        tiles = tiles[::-1]
    total = tiles[0]
    for tile in tiles[1:]:
        total = total * F32(ratio**8) + tile
    return jnp.sum(total * weights, axis=0, keepdims=True)


def face_kernel(f_hbm, f, y_down, y_up, sems):
    planes, _, cols = f.shape
    steps = planes // group
    for i in range(steps):
        part = pl.ds(i * group, group)
        pltpu.make_async_copy(f_hbm.at[part], f.at[part], sems.at[i]).start()
    ty = y_functionals(cols)

    def step(i, carry):
        part = pl.ds(i * group, group)
        pltpu.make_async_copy(f_hbm.at[part], f.at[part], sems.at[i]).wait()
        for j in range(group):
            p = i * group + j
            row = pl.ds(p, 1)
            both = jnp.concatenate(split(f[p]), axis=-1)
            r = dot(ty, both, ((1,), (1,)))
            r = r[:16] + r[16:]
            for k in range(6):
                y_down[k, row, :] = r[k : k + 1]
                y_up[k, row, :] = r[8 + k : 9 + k]
        return carry

    lax.fori_loop(0, steps, step, 0)


def x_local_kernel(f, w, dx_out, fx, dx_low, dx_high, x_down, x_up, dx, sems):
    planes, n, cols = f.shape
    pairs = group // 2
    deriv, smooth = line_operators()
    at = lax.broadcasted_iota(jnp.int32, (8, cols), 0)
    f_head, f_tail = powers_of(smooth.ratio, at, 3), powers_of(smooth.ratio, 7 - at, 3)
    d_head, d_tail = powers_of(deriv.ratio, at, 3), powers_of(deriv.ratio, 7 - at, 3)
    inner = pl.ds(deriv_rim, n - 2 * deriv_rim)

    def written(i):
        part = pl.ds(i * group, group)
        return pltpu.make_async_copy(dx.at[part, inner], dx_out.at[part, inner], sems.at[i])

    def step(i, carry):
        for j in range(pairs):
            p = i * group + 2 * j
            hi, lo = split(jnp.concatenate([f[p], f[p + 1]], axis=-1))
            r = dot(w[:, :n], hi) + dot(w[:, n:], hi) + dot(w[:, :n], lo)
            for half in range(2):
                q = p + half
                at = slice(128 * half, 128 * half + 128)
                dx[q] = r[:n, at]
                dx_low[q] = r[:deriv_rim, at]
                dx_high[q] = r[n - deriv_rim : n, at]
                fx[q] = r[n:, at]
                row = pl.ds(q, 1)
                x_down[0, row, :] = geometric(f[q, :reach, :], smooth.ratio, f_head, False)
                x_up[0, row, :] = geometric(f[q, n - reach :, :], smooth.ratio, f_tail, True)
                x_down[5, row, :] = geometric(f[q, : reach // 2, :], deriv.ratio, d_head, False)
                x_up[5, row, :] = geometric(f[q, n - reach // 2 :, :], deriv.ratio, d_tail, True)
                for k in range(4):
                    x_down[1 + k, row, :] = f[q, k : k + 1, :]
                    x_up[1 + k, row, :] = f[q, n - 4 + k : n - 3 + k, :]
        written(i).start()
        return carry

    lax.fori_loop(0, planes // group, step, 0)
    for i in range(planes // group):
        written(i).wait()


def dot3(rows, hi, lo):
    a, b = split(rows)
    return dot(a, hi) + dot(a, lo) + dot(b, hi)


def x_face_kernel(x_down, x_up, lower, upper, by, tx, vy, down, up):
    planes = lower.shape[1]
    n = by.shape[1] // 2
    rows = jnp.concatenate([x_down[k] for k in range(5)] + [x_up[k] for k in range(5)], axis=0)
    own = dot3(rows, by[:, :n], by[:, n:])
    rows = jnp.concatenate([lower[g] for g in range(5)] + [upper[g] for g in range(5)], axis=0)
    r = dot3(rows, tx[:, :128], tx[:, 128:])
    z = r[:planes]
    for g in range(1, 10):
        z = z + pltpu.roll(r[g * planes : (g + 1) * planes], 10 * g, 1)
    rows = jnp.concatenate([z] + [pltpu.roll(z, 128 - k, 1) for k in range(1, 10)], axis=0)
    own = own + dot3(rows, vy[:, :n], vy[:, n:])
    for k in range(5):
        down[k] = own[k * planes : (k + 1) * planes]
        up[k] = own[(5 + k) * planes : (6 + k) * planes]
    down[5] = x_down[5]
    up[5] = x_up[5]
    down[6] = x_down[1]
    up[6] = x_up[4]


def y_kernel(f, fx, lower, upper, ax, v, wy_d, wy_f, dy_out, sm_out, sm_low, sm_high, halo, dy, sm, sems):
    planes, n, _ = f.shape
    rows = jnp.concatenate([lower[k] for k in range(5)] + [upper[k] for k in range(5)], axis=0)
    filtered = dot3(rows, ax[:, :n], ax[:, n:])
    zero = jnp.zeros((planes, n), F32)
    table = [filtered[k * planes : (k + 1) * planes] for k in range(5)] + [lower[5], lower[4], zero]
    table += [filtered[(5 + k) * planes : (6 + k) * planes] for k in range(5)] + [upper[5], upper[1], zero]
    for k in range(16):
        for c in range(0, n, 128):
            halo[c // 128, pl.ds(k, planes, stride=16), :] = table[k][:, c : c + 128]
    inner = pl.ds(filter_rim, n - 2 * filter_rim)

    def written(i):
        part = pl.ds(i * group, group)
        return (
            pltpu.make_async_copy(dy.at[part], dy_out.at[part], sems.at[0, i]),
            pltpu.make_async_copy(sm.at[part, inner], sm_out.at[part, inner], sems.at[1, i]),
        )

    def step(i, carry):
        for j in range(group):
            p = i * group + j
            at = pl.ds(pl.multiple_of(p * 16, 16), 16)
            hi, lo = split(jnp.concatenate([halo[c, at, :] for c in range(n // 128)], axis=-1))
            r = dot(jnp.concatenate([hi, lo, hi], axis=0), v[...], ((0,), (0,)))
            d = dot(jnp.concatenate(split(f[p]), axis=-1), wy_d[...])
            dy[p] = d[:, :128] + d[:, 128:] + r[:, :128]
            s = dot(jnp.concatenate(split(fx[p]), axis=-1), wy_f[...])
            s = s[:, :128] + s[:, 128:] + r[:, 128:]
            sm[p] = s
            sm_low[p] = s[:filter_rim]
            sm_high[p] = s[n - filter_rim :]
        for copy in written(i):
            copy.start()
        return carry

    lax.fori_loop(0, planes // group, step, 0)
    for i in range(planes // group):
        for copy in written(i):
            copy.wait()


def rim_kernel(
    dx_low, dx_high, sm_low, sm_high, lower, upper, ds_low, ds_high, dc_low, dc_high, fs_low, fs_high, fc_low, fc_high,
    dx_in, sm_in, dx_out, sm_out, dl, dh, sl, sh, sems,
):
    planes = dx_low.shape[0]
    n = dx_out.shape[1]

    def written(i):
        part = pl.ds(i * group, group)
        return (
            pltpu.make_async_copy(dl.at[part], dx_out.at[part, pl.ds(0, deriv_rim)], sems.at[0, i]),
            pltpu.make_async_copy(dh.at[part], dx_out.at[part, pl.ds(n - deriv_rim, deriv_rim)], sems.at[1, i]),
            pltpu.make_async_copy(sl.at[part], sm_out.at[part, pl.ds(0, filter_rim)], sems.at[2, i]),
            pltpu.make_async_copy(sh.at[part], sm_out.at[part, pl.ds(n - filter_rim, filter_rim)], sems.at[3, i]),
        )

    def step(i, carry):
        for j in range(group):
            p = i * group + j
            row = pl.ds(p, 1)
            low = dx_low[p] + ds_low[...] * lower[5, row, :]
            high = dx_high[p] + ds_high[...] * upper[5, row, :]
            dl[p] = jnp.concatenate([low[:8] + dc_low[...] * lower[6, row, :], low[8:]], axis=0)
            dh[p] = jnp.concatenate([high[:-8], high[-8:] + dc_high[...] * upper[6, row, :]], axis=0)
            low = sm_low[p] + fs_low[...] * lower[0, row, :]
            high = sm_high[p] + fs_high[...] * upper[0, row, :]
            near_low, near_high = low[:8], high[-8:]
            for k in range(4):
                near_low = near_low + fc_low[k] * lower[1 + k, row, :]
                near_high = near_high + fc_high[k] * upper[1 + k, row, :]
            sl[p] = jnp.concatenate([near_low, low[8:]], axis=0)
            sh[p] = jnp.concatenate([high[:-8], near_high], axis=0)
        for copy in written(i):
            copy.start()
        return carry

    lax.fori_loop(0, planes // group, step, 0)
    for i in range(planes // group):
        for copy in written(i):
            copy.wait()


def tables(rows, cols):
    deriv, smooth = line_operators()
    t = {}
    for name, line in (("d", deriv), ("f", smooth)):
        hi, lo = halves(line.block(rows))
        t["wx_" + name] = np.concatenate([hi, lo], axis=1)
        hi, lo = halves(line.block(cols).T)
        t["wy_" + name] = np.block([[hi, lo], [hi, np.zeros_like(lo)]])
    hi, lo = halves(smooth.block(rows).T)
    t["ax"] = np.concatenate([hi, lo], axis=1)
    t["wx"] = np.concatenate([t.pop("wx_d"), t.pop("wx_f")], axis=0)
    powers = lambda line, count: line.ratio ** np.arange(count)
    hi, lo = halves(smooth.block(cols).T)
    t["by"] = np.concatenate([hi, lo], axis=1)
    tx = np.zeros((rows, 128))
    tx[:, 0] = powers(smooth, rows)
    tx[:, 5] = tx[::-1, 0]
    for k in range(4):
        tx[k, 1 + k] = 1.0
        tx[rows - 4 + k, 6 + k] = 1.0
    hi, lo = halves(tx)
    t["tx"] = np.concatenate([hi, lo], axis=1)
    low, high = smooth.from_below(cols), smooth.from_above(cols)
    vy = np.zeros((128, cols))
    for g in range(5):
        vy[10 * g] = low[:, g]
        vy[10 * (5 + g)] = high[:, g]
    hi, lo = halves(vy)
    t["vy"] = np.concatenate([hi, lo], axis=1)
    low, high = smooth.from_below(rows), smooth.from_above(rows)
    t["fs_low"], t["fs_high"] = lanes(low[:filter_rim, 0]), lanes(high[-filter_rim:, 0])
    t["fc_low"] = np.stack([lanes(low[:8, 1 + k]) for k in range(4)])
    t["fc_high"] = np.stack([lanes(high[-8:, 1 + k]) for k in range(4)])
    low, high = deriv.from_below(rows), deriv.from_above(rows)
    t["ds_low"], t["ds_high"] = lanes(low[:deriv_rim, 0]), lanes(high[-deriv_rim:, 0])
    t["dc_low"], t["dc_high"] = lanes(low[:8, 4]), lanes(high[-8:, 1])
    v = np.zeros((16, 2 * cols))
    low, high = smooth.from_below(cols), smooth.from_above(cols)
    v[0:5, cols:], v[8:13, cols:] = low.T, high.T
    low, high = deriv.from_below(cols), deriv.from_above(cols)
    v[5, :cols], v[6, :cols] = low[:, 0], low[:, 4]
    v[13, :cols], v[14, :cols] = high[:, 0], high[:, 1]
    hi, lo = halves(v)
    t["v"] = np.concatenate([hi, hi, lo], axis=0)
    return {key: jnp.asarray(value) for key, value in t.items()}


def shifted(values, axis, by):
    count = lax.axis_size(axis)
    return lax.ppermute(values, axis, [(i, (i + by) % count) for i in range(count)])


def on_device(fields):
    shape = fields.shape
    rows, cols = shape[2:]
    planes = shape[0] * shape[1]
    block = (planes, rows, cols)
    t = tables(rows, cols)
    steps = planes // group
    x_face, y_face = (6, planes, cols), (6, planes, rows)
    dx_rim, sm_rim = (planes, deriv_rim, cols), (planes, filter_rim, cols)
    f, y_down, y_up = call(
        "faces", face_kernel, [block, y_face, y_face],
        [pltpu.with_memory_space_constraint(fields.reshape(block), pltpu.HBM)], 10**9, 10**7,
        in_specs=[ANY], scratch=[pltpu.SemaphoreType.DMA((steps,))],
    )
    y_lower = shifted(y_up, "gy", 1)
    y_upper = shifted(y_down, "gy", -1)
    dx, fx, dx_low, dx_high, x_down, x_up = call(
        "x_local", x_local_kernel, [block, block, dx_rim, dx_rim, x_face, x_face], [f, t["wx"]], 4 * 10**9, 10**7,
        out_specs=[ANY] + [VMEM] * 5,
        scratch=[pltpu.VMEM(block, F32), pltpu.SemaphoreType.DMA((steps,))],
    )
    face = (7, planes, cols)
    x_down, x_up = call(
        "x_faces", x_face_kernel, [face, face],
        [x_down, x_up, y_lower, y_upper, t["by"], t["tx"], t["vy"]], 10**8, 10**6,
    )
    x_lower = shifted(x_up, "gx", 1)
    x_upper = shifted(x_down, "gx", -1)
    dy, sm, sm_low, sm_high = call(
        "y_all", y_kernel, [block, block, sm_rim, sm_rim],
        [f, fx, y_lower, y_upper] + [t[k] for k in ("ax", "v", "wy_d", "wy_f")], 6 * 10**9, 2 * 10**7,
        out_specs=[ANY, ANY, VMEM, VMEM],
        scratch=[
            pltpu.VMEM((rows // 128, planes * 16, 128), F32),
            pltpu.VMEM(block, F32),
            pltpu.VMEM(block, F32),
            pltpu.SemaphoreType.DMA((2, steps)),
        ],
        limit=24,
    )
    rims = ("ds_low", "ds_high", "dc_low", "dc_high", "fs_low", "fs_high", "fc_low", "fc_high")
    ins = [dx_low, dx_high, sm_low, sm_high, x_lower, x_upper] + [t[k] for k in rims]
    dx, sm = call(
        "rims", rim_kernel, [block, block], ins + [dx, sm], 10**8, 4 * 10**6,
        in_specs=[VMEM] * len(ins) + [ANY, ANY],
        out_specs=[ANY, ANY],
        scratch=[pltpu.VMEM(shape, F32) for shape in (dx_rim, dx_rim, sm_rim, sm_rim)]
        + [pltpu.SemaphoreType.DMA((4, steps))],
        aliases={len(ins): 0, len(ins) + 1: 1},
    )
    return tuple(out.reshape(shape) for out in (dx, dy, sm))


def solution(mesh):
    placed = P(None, None, "gx", "gy")
    return jax.shard_map(
        on_device, mesh=mesh, in_specs=(placed,), out_specs=(placed, placed, placed), check_vma=False
    )
```

```python
import math

import jax
import jax.numpy as jnp
import ml_dtypes
import numpy as np
from jax import lax
from jax.experimental import pallas as pl
from jax.experimental.pallas import tpu as pltpu
from jax.sharding import PartitionSpec as P

F32 = jnp.float32
BF16 = jnp.bfloat16
deriv_offdiag = 1.0 / 3.0
coef_near = 14.0 / 9.0
coef_far = 1.0 / 9.0
filter_offdiag = 0.45
reach = 64
filter_rim = 40
deriv_rim = 24
group = 8
pieces = ((0, 8), (8, 8), (16, 8), (24, 8), (32, 8))
span = 40
chunk = 4


def filter_weights():
    return [
        (193.0 + 126.0 * filter_offdiag) / 256.0,
        (105.0 + 302.0 * filter_offdiag) / 256.0,
        15.0 * (2.0 * filter_offdiag - 1.0) / 64.0,
        45.0 * (1.0 - 2.0 * filter_offdiag) / 512.0,
        5.0 * (2.0 * filter_offdiag - 1.0) / 256.0,
        (1.0 - 2.0 * filter_offdiag) / 512.0,
    ]


class Line:
    def __init__(self, offdiag, taps, sign, width):
        gap = math.sqrt(1.0 - 4.0 * offdiag * offdiag)
        self.ratio = (gap - 1.0) / (2.0 * offdiag)
        self.gap = gap
        self.taps = taps
        self.sign = sign
        far = width + 4
        self.scale = self.tap(far) / self.ratio**far
        self.near = [0.0] + [
            self.tap(n) - self.scale * self.ratio**n if n <= width else 0.0 for n in range(1, 2 * far)
        ]

    def tap(self, n):
        return sum(w * self.ratio ** abs(n - o) / self.gap for o, w in self.taps)

    def block(self, cells):
        values = np.array([self.tap(n) for n in range(-cells + 1, cells)])
        ids = np.arange(cells)
        return values[ids[None, :] - ids[:, None] + cells - 1]

    def near_at(self, n):
        return self.near[n] if 0 < n < len(self.near) else 0.0

    def from_below(self, cells):
        table = np.zeros((cells, 5))
        for i in range(cells):
            table[i, 0] = self.sign * self.scale * self.ratio ** (i + 1)
            for k in range(4):
                table[i, 1 + k] = self.sign * self.near_at(i + 4 - k)
        return table

    def from_above(self, cells):
        table = np.zeros((cells, 5))
        for i in range(cells):
            table[i, 0] = self.scale * self.ratio ** (cells - i)
            for k in range(4):
                table[i, 1 + k] = self.near_at(cells + k - i)
        return table


def line_operators():
    weights = filter_weights()
    deriv_taps = [
        (-2, -coef_far / 4.0),
        (-1, -coef_near / 2.0),
        (1, coef_near / 2.0),
        (2, coef_far / 4.0),
    ]
    filter_taps = [(0, weights[0])]
    for order in range(1, 6):
        filter_taps.append((order, weights[order] / 2.0))
        filter_taps.append((-order, weights[order] / 2.0))
    return Line(deriv_offdiag, deriv_taps, -1.0, 1), Line(filter_offdiag, filter_taps, 1.0, 4)


def halves(table):
    hi = np.asarray(table, np.float32).astype(ml_dtypes.bfloat16)
    lo = (np.asarray(table, np.float64) - hi.astype(np.float64)).astype(ml_dtypes.bfloat16)
    return hi, lo


def split(values):
    hi = values.astype(BF16)
    return hi, (values - hi.astype(F32)).astype(BF16)


def dot(a, b, dims=((1,), (0,))):
    return lax.dot_general(a, b, (dims, ((), ())), preferred_element_type=F32)


def lanes(column):
    return np.repeat(np.asarray(column, np.float32)[:, None], 128, axis=1)


VMEM = pl.BlockSpec(memory_space=pltpu.VMEM)
ANY = pl.BlockSpec(memory_space=pl.ANY)


def call(name, kernel, outs, ins, flops, nbytes, in_specs=None, out_specs=None, scratch=(), limit=20, aliases=None):
    return pl.pallas_call(
        kernel,
        in_specs=in_specs or [VMEM] * len(ins),
        out_specs=out_specs or [VMEM] * len(outs),
        out_shape=[jax.ShapeDtypeStruct(shape, F32) for shape in outs],
        scratch_shapes=list(scratch),
        input_output_aliases=aliases or {},
        compiler_params=pltpu.CompilerParams(vmem_limit_bytes=limit << 20),
        cost_estimate=pl.CostEstimate(flops=flops, bytes_accessed=nbytes, transcendentals=0),
        name=name,
    )(*ins)


def powers_of(ratio, exponent, bits):
    out = jnp.where(exponent & 1 == 1, F32(ratio), F32(1.0))
    for b in range(1, bits):
        out = out * jnp.where((exponent >> b) & 1 == 1, F32(ratio ** (1 << b)), F32(1.0))
    return out


def y_functionals(cols):
    deriv, smooth = line_operators()
    shape = (8, cols)
    at = lax.broadcasted_iota(jnp.int32, shape, 1)
    row = lax.broadcasted_iota(jnp.int32, shape, 0)
    parts = []
    for place, first in ((at, at - (row - 1)), (cols - 1 - at, at - (cols - 5 + row))):
        cell = jnp.where((first == 0) & (row >= 1) & (row <= 4), F32(1.0), F32(0.0))
        cell = jnp.where(row == 0, powers_of(smooth.ratio, place, 7), cell)
        parts.append(jnp.where(row == 5, powers_of(deriv.ratio, place, 7), cell))
    hi, lo = split(jnp.concatenate(parts, axis=0))
    return jnp.concatenate(
        [jnp.concatenate([hi, hi], axis=1), jnp.concatenate([lo, jnp.zeros_like(lo)], axis=1)], axis=0
    )


def geometric(values, ratio, weights, tail):
    tiles = [values[8 * j : 8 * j + 8] for j in range(values.shape[0] // 8)]
    if not tail:
        tiles = tiles[::-1]
    total = tiles[0]
    for tile in tiles[1:]:
        total = total * F32(ratio**8) + tile
    return jnp.sum(total * weights, axis=0, keepdims=True)


def face_kernel(f_hbm, f, y_down, y_up, sems):
    cols = f.shape[2]
    reads = []
    for i, (first, planes) in enumerate(pieces):
        part = pl.ds(first, planes)
        reads.append(pltpu.make_async_copy(f_hbm.at[part], f.at[part], sems.at[i]))
        reads[-1].start()
    ty = y_functionals(cols)
    for read, (first, planes) in zip(reads, pieces):
        read.wait()
        for p in range(first, first + planes):
            both = jnp.concatenate(split(f[p]), axis=-1)
            r = dot(ty, both, ((1,), (1,)))
            r = r[:16] + r[16:]
            for k in range(6):
                y_down[k, p : p + 1, :] = r[k : k + 1]
                y_up[k, p : p + 1, :] = r[8 + k : 9 + k]


def windows(cells, margin):
    pieces, first = [], 0
    while first < cells:
        start = min(max(0, (first - margin) // 16 * 16), cells - 128)
        end = cells if start == cells - 128 else (start + 128 - margin) // 8 * 8
        pieces.append((first, end - first, start))
        first = end
    return pieces


def window_weights(line, cells, margin):
    block = line.block(cells)
    tables = []
    for first, count, start in windows(cells, margin):
        hi, lo = halves(block[first : first + count, start : start + 128])
        tables.append(np.block([[hi, hi], [lo, np.zeros_like(lo)]]))
    return np.concatenate(tables, axis=0)


def x_operator(hi, lo, w, margin):
    parts = []
    for first, count, start in windows(hi.shape[0], margin):
        cells = jnp.concatenate([hi[start : start + 128], lo[start : start + 128]], axis=0)
        r = dot(w[2 * first : 2 * (first + count)], cells)
        parts.append(r[:count] + r[count:])
    r = jnp.concatenate(parts, axis=0)
    return r[:, :128], r[:, 128:]


def sweep(planes, body, written):
    def step(i, carry):
        for j in range(0, span, 2):
            body(i * span + j)
            if (j + 2) % chunk == 0:
                for copy in written(i * (span // chunk) + j // chunk):
                    copy.start()
        return carry

    lax.fori_loop(0, planes // span, step, 0)
    for i in range(planes // chunk):
        for copy in written(i):
            copy.wait()


def local_kernel(f, wx, wy, dx_out, part_y, dx_low, dx_high, down, up, dx, sems):
    planes, n, cols = f.shape
    deriv, _ = line_operators()
    at = lax.broadcasted_iota(jnp.int32, (8, cols), 0)
    head, tail = powers_of(deriv.ratio, at, 3), powers_of(deriv.ratio, 7 - at, 3)
    inner = pl.ds(deriv_rim, n - 2 * deriv_rim)

    def written(i):
        part = pl.ds(i * chunk, chunk)
        return (pltpu.make_async_copy(dx.at[part, inner], dx_out.at[part, inner], sems.at[i]),)

    def body(p):
        hi, lo = split(jnp.concatenate([f[p], f[p + 1]], axis=-1))
        for j, r in enumerate(x_operator(hi, lo, wx, deriv_rim)):
            q = p + j
            at = slice(cols * j, cols * j + cols)
            part_y[q] = dot(jnp.concatenate([hi[:, at], lo[:, at]], axis=-1), wy[...])
            dx[q] = r
            dx_low[q] = r[:deriv_rim]
            dx_high[q] = r[n - deriv_rim :]
            row = pl.ds(q, 1)
            down[0, row, :] = geometric(f[q, : reach // 2, :], deriv.ratio, head, False)
            up[0, row, :] = geometric(f[q, n - reach // 2 :, :], deriv.ratio, tail, True)
            down[1, row, :] = f[q, 0:1, :]
            up[1, row, :] = f[q, n - 1 : n, :]

    sweep(planes, body, written)


def y_kernel(f, part_y, lower, upper, d_down, d_up, w, dy, gy, down, up, halo):
    planes, n, cols = f.shape
    _, smooth = line_operators()
    zero = jnp.zeros((planes, 128), F32)
    for c in range(0, n, 128):
        for k in range(16):
            rows = lower[k, :, c : c + 128] if k < 6 else upper[k - 6, :, c : c + 128] if k < 12 else zero
            halo[c // 128, pl.ds(k, planes, stride=16), :] = rows
    for k in range(2):
        down[5 + k] = d_down[k]
        up[5 + k] = d_up[k]
    at = lax.broadcasted_iota(jnp.int32, (8, cols), 0)
    head, tail = powers_of(smooth.ratio, at, 3), powers_of(smooth.ratio, 7 - at, 3)

    def step(i, carry):
        for j in range(span):
            q = i * span + j
            at = pl.ds(pl.multiple_of(q * 16, 16), 16)
            hi, lo = split(jnp.concatenate([halo[c, at, :] for c in range(n // 128)], axis=-1))
            faces = jnp.concatenate([hi, lo, hi], axis=0).T
            r = dot(jnp.concatenate([f[q].astype(BF16), faces], axis=-1), w[...]) + part_y[q]
            dy[q] = r[:, :128]
            g = r[:, 128:]
            gy[q] = g
            row = pl.ds(q, 1)
            down[0, row, :] = geometric(g[:reach], smooth.ratio, head, False)
            up[0, row, :] = geometric(g[n - reach :], smooth.ratio, tail, True)
            for k in range(4):
                down[1 + k, row, :] = g[k : k + 1]
                up[1 + k, row, :] = g[n - 4 + k : n - 3 + k]
        return carry

    lax.fori_loop(0, planes // span, step, 0)


def x_filter_kernel(gy, dy, w, dy_out, sm_out, sm_low, sm_high, sm, sems):
    planes, n, _ = gy.shape
    inner = pl.ds(filter_rim, n - 2 * filter_rim)

    def written(i):
        part = pl.ds(i * chunk, chunk)
        return (
            pltpu.make_async_copy(sm.at[part, inner], sm_out.at[part, inner], sems.at[0, i]),
            pltpu.make_async_copy(dy.at[part], dy_out.at[part], sems.at[1, i]),
        )

    def body(p):
        hi, lo = split(jnp.concatenate([gy[p], gy[p + 1]], axis=-1))
        for j, r in enumerate(x_operator(hi, lo, w, filter_rim)):
            sm[p + j] = r
            sm_low[p + j] = r[:filter_rim]
            sm_high[p + j] = r[n - filter_rim :]

    sweep(planes, body, written)


def rim_kernel(
    dx_low, dx_high, sm_low, sm_high, lower, upper, ds_low, ds_high, dc_low, dc_high, fs_low, fs_high, fc_low, fc_high,
    dx_in, sm_in, dx_out, sm_out, dl, dh, sl, sh, sems,
):
    planes = dx_low.shape[0]
    n = dx_out.shape[1]

    def written(i):
        part = pl.ds(i * group, group)
        return (
            pltpu.make_async_copy(dl.at[part], dx_out.at[part, pl.ds(0, deriv_rim)], sems.at[0, i]),
            pltpu.make_async_copy(dh.at[part], dx_out.at[part, pl.ds(n - deriv_rim, deriv_rim)], sems.at[1, i]),
            pltpu.make_async_copy(sl.at[part], sm_out.at[part, pl.ds(0, filter_rim)], sems.at[2, i]),
            pltpu.make_async_copy(sh.at[part], sm_out.at[part, pl.ds(n - filter_rim, filter_rim)], sems.at[3, i]),
        )

    def step(i, carry):
        for j in range(group):
            p = i * group + j
            row = pl.ds(p, 1)
            low = dx_low[p] + ds_low[...] * lower[5, row, :]
            high = dx_high[p] + ds_high[...] * upper[5, row, :]
            dl[p] = jnp.concatenate([low[:8] + dc_low[...] * lower[6, row, :], low[8:]], axis=0)
            dh[p] = jnp.concatenate([high[:-8], high[-8:] + dc_high[...] * upper[6, row, :]], axis=0)
            low = sm_low[p] + fs_low[...] * lower[0, row, :]
            high = sm_high[p] + fs_high[...] * upper[0, row, :]
            near_low, near_high = low[:8], high[-8:]
            for k in range(4):
                near_low = near_low + fc_low[k] * lower[1 + k, row, :]
                near_high = near_high + fc_high[k] * upper[1 + k, row, :]
            sl[p] = jnp.concatenate([near_low, low[8:]], axis=0)
            sh[p] = jnp.concatenate([high[:-8], near_high], axis=0)
        for copy in written(i):
            copy.start()
        return carry

    lax.fori_loop(0, planes // group, step, 0)
    for i in range(planes // group):
        for copy in written(i):
            copy.wait()


def tables(rows, cols):
    deriv, smooth = line_operators()
    t = {"wx_d": window_weights(deriv, rows, deriv_rim), "wx_f": window_weights(smooth, rows, filter_rim)}
    d_hi, d_lo = halves(deriv.block(cols).T)
    f_hi, f_lo = halves(smooth.block(cols).T)
    hi, lo = np.concatenate([d_hi, f_hi], axis=1), np.concatenate([d_lo, f_lo], axis=1)
    v = np.zeros((16, 2 * cols))
    low, high = smooth.from_below(cols), smooth.from_above(cols)
    v[0:5, cols:], v[6:11, cols:] = low.T, high.T
    low, high = deriv.from_below(cols), deriv.from_above(cols)
    v[5, :cols], v[4, :cols] = low[:, 0], low[:, 4]
    v[11, :cols], v[7, :cols] = high[:, 0], high[:, 1]
    v_hi, v_lo = halves(v)
    t["wy"] = np.concatenate([hi, hi], axis=0)
    t["wy_more"] = np.concatenate([lo, v_hi, v_hi, v_lo], axis=0)
    low, high = smooth.from_below(rows), smooth.from_above(rows)
    t["fs_low"], t["fs_high"] = lanes(low[:filter_rim, 0]), lanes(high[-filter_rim:, 0])
    t["fc_low"] = np.stack([lanes(low[:8, 1 + k]) for k in range(4)])
    t["fc_high"] = np.stack([lanes(high[-8:, 1 + k]) for k in range(4)])
    low, high = deriv.from_below(rows), deriv.from_above(rows)
    t["ds_low"], t["ds_high"] = lanes(low[:deriv_rim, 0]), lanes(high[-deriv_rim:, 0])
    t["dc_low"], t["dc_high"] = lanes(low[:8, 4]), lanes(high[-8:, 1])
    return {key: jnp.asarray(value) for key, value in t.items()}


def shifted(values, axis, by):
    count = lax.axis_size(axis)
    return lax.ppermute(values, axis, [(i, (i + by) % count) for i in range(count)])


def on_device(fields):
    shape = fields.shape
    rows, cols = shape[2:]
    planes = shape[0] * shape[1]
    block = (planes, rows, cols)
    t = tables(rows, cols)
    steps = planes // group
    y_face = (6, planes, rows)
    dx_rim, sm_rim = (planes, deriv_rim, cols), (planes, filter_rim, cols)
    f, y_down, y_up = call(
        "faces", face_kernel, [block, y_face, y_face],
        [pltpu.with_memory_space_constraint(fields.reshape(block), pltpu.HBM)], 10**9, 10**7,
        in_specs=[ANY], scratch=[pltpu.SemaphoreType.DMA((len(pieces),))],
    )
    y_lower = shifted(y_up, "gy", 1)
    y_upper = shifted(y_down, "gy", -1)
    few, face = (2, planes, cols), (7, planes, cols)
    copies = planes // chunk
    dx, part_y, dx_low, dx_high, d_down, d_up = call(
        "local", local_kernel, [block, (planes, rows, 2 * cols), dx_rim, dx_rim, few, few],
        [f, t["wx_d"], t["wy"]], 4 * 10**9, 10**7,
        out_specs=[ANY] + [VMEM] * 5, scratch=[pltpu.VMEM(block, F32), pltpu.SemaphoreType.DMA((copies,))],
    )
    dy, gy, x_down, x_up = call(
        "y_both", y_kernel, [block, block, face, face],
        [f, part_y, y_lower, y_upper, d_down, d_up, t["wy_more"]], 6 * 10**9, 2 * 10**7,
        scratch=[pltpu.VMEM((rows // 128, planes * 16, 128), F32)],
    )
    x_lower = shifted(x_up, "gx", 1)
    x_upper = shifted(x_down, "gx", -1)
    dy, sm, sm_low, sm_high = call(
        "x_filter", x_filter_kernel, [block, block, sm_rim, sm_rim], [gy, dy, t["wx_f"]], 4 * 10**9, 10**7,
        out_specs=[ANY, ANY, VMEM, VMEM],
        scratch=[pltpu.VMEM(block, F32), pltpu.SemaphoreType.DMA((2, copies))],
    )
    rims = ("ds_low", "ds_high", "dc_low", "dc_high", "fs_low", "fs_high", "fc_low", "fc_high")
    ins = [dx_low, dx_high, sm_low, sm_high, x_lower, x_upper] + [t[k] for k in rims]
    dx, sm = call(
        "rims", rim_kernel, [block, block], ins + [dx, sm], 10**8, 4 * 10**6,
        in_specs=[VMEM] * len(ins) + [ANY, ANY],
        out_specs=[ANY, ANY],
        scratch=[pltpu.VMEM(shape, F32) for shape in (dx_rim, dx_rim, sm_rim, sm_rim)]
        + [pltpu.SemaphoreType.DMA((4, steps))],
        aliases={len(ins): 0, len(ins) + 1: 1},
    )
    return tuple(out.reshape(shape) for out in (dx, dy, sm))


def solution(mesh):
    placed = P(None, None, "gx", "gy")
    return jax.shard_map(
        on_device, mesh=mesh, in_specs=(placed,), out_specs=(placed, placed, placed), check_vma=False
    )
```

```python
import math

import jax
import jax.numpy as jnp
import ml_dtypes
import numpy as np
from jax import lax
from jax.experimental import pallas as pl
from jax.experimental.pallas import tpu as pltpu
from jax.sharding import PartitionSpec as P

F32 = jnp.float32
BF16 = jnp.bfloat16
deriv_offdiag = 1.0 / 3.0
coef_near = 14.0 / 9.0
coef_far = 1.0 / 9.0
filter_offdiag = 0.45
reach = 64
filter_rim = 40
deriv_rim = 24
pieces = ((0, 8), (8, 8), (16, 8), (24, 8), (32, 8))
chunk = 4
lag = 8
rim_chunk = 8


def filter_weights():
    return [
        (193.0 + 126.0 * filter_offdiag) / 256.0,
        (105.0 + 302.0 * filter_offdiag) / 256.0,
        15.0 * (2.0 * filter_offdiag - 1.0) / 64.0,
        45.0 * (1.0 - 2.0 * filter_offdiag) / 512.0,
        5.0 * (2.0 * filter_offdiag - 1.0) / 256.0,
        (1.0 - 2.0 * filter_offdiag) / 512.0,
    ]


class Line:
    def __init__(self, offdiag, taps, sign, width):
        gap = math.sqrt(1.0 - 4.0 * offdiag * offdiag)
        self.ratio = (gap - 1.0) / (2.0 * offdiag)
        self.gap = gap
        self.taps = taps
        self.sign = sign
        far = width + 4
        self.scale = self.tap(far) / self.ratio**far
        self.near = [0.0] + [
            self.tap(n) - self.scale * self.ratio**n if n <= width else 0.0 for n in range(1, 2 * far)
        ]

    def tap(self, n):
        return sum(w * self.ratio ** abs(n - o) / self.gap for o, w in self.taps)

    def block(self, cells):
        values = np.array([self.tap(n) for n in range(-cells + 1, cells)])
        ids = np.arange(cells)
        return values[ids[None, :] - ids[:, None] + cells - 1]

    def near_at(self, n):
        return self.near[n] if 0 < n < len(self.near) else 0.0

    def from_below(self, cells):
        table = np.zeros((cells, 5))
        for i in range(cells):
            table[i, 0] = self.sign * self.scale * self.ratio ** (i + 1)
            for k in range(4):
                table[i, 1 + k] = self.sign * self.near_at(i + 4 - k)
        return table

    def from_above(self, cells):
        table = np.zeros((cells, 5))
        for i in range(cells):
            table[i, 0] = self.scale * self.ratio ** (cells - i)
            for k in range(4):
                table[i, 1 + k] = self.near_at(cells + k - i)
        return table


def line_operators():
    weights = filter_weights()
    deriv_taps = [
        (-2, -coef_far / 4.0),
        (-1, -coef_near / 2.0),
        (1, coef_near / 2.0),
        (2, coef_far / 4.0),
    ]
    filter_taps = [(0, weights[0])]
    for order in range(1, 6):
        filter_taps.append((order, weights[order] / 2.0))
        filter_taps.append((-order, weights[order] / 2.0))
    return Line(deriv_offdiag, deriv_taps, -1.0, 1), Line(filter_offdiag, filter_taps, 1.0, 4)


def halves(table):
    hi = np.asarray(table, np.float32).astype(ml_dtypes.bfloat16)
    lo = (np.asarray(table, np.float64) - hi.astype(np.float64)).astype(ml_dtypes.bfloat16)
    return hi, lo


def split(values):
    hi = values.astype(BF16)
    return hi, (values - hi.astype(F32)).astype(BF16)


def dot(a, b, dims=((1,), (0,))):
    return lax.dot_general(a, b, (dims, ((), ())), preferred_element_type=F32)


def lanes(column):
    return np.repeat(np.asarray(column, np.float32)[:, None], 128, axis=1)


VMEM = pl.BlockSpec(memory_space=pltpu.VMEM)
ANY = pl.BlockSpec(memory_space=pl.ANY)


def call(name, kernel, outs, ins, flops, nbytes, in_specs=None, out_specs=None, scratch=(), limit=20, aliases=None):
    return pl.pallas_call(
        kernel,
        in_specs=in_specs or [VMEM] * len(ins),
        out_specs=out_specs or [VMEM] * len(outs),
        out_shape=[jax.ShapeDtypeStruct(shape, F32) for shape in outs],
        scratch_shapes=list(scratch),
        input_output_aliases=aliases or {},
        compiler_params=pltpu.CompilerParams(vmem_limit_bytes=limit << 20),
        cost_estimate=pl.CostEstimate(flops=flops, bytes_accessed=nbytes, transcendentals=0),
        name=name,
    )(*ins)


def powers_of(ratio, exponent, bits):
    out = jnp.where(exponent & 1 == 1, F32(ratio), F32(1.0))
    for b in range(1, bits):
        out = out * jnp.where((exponent >> b) & 1 == 1, F32(ratio ** (1 << b)), F32(1.0))
    return out


def y_functionals(cols):
    deriv, smooth = line_operators()
    shape = (8, cols)
    at = lax.broadcasted_iota(jnp.int32, shape, 1)
    row = lax.broadcasted_iota(jnp.int32, shape, 0)
    parts = []
    for place, first in ((at, at - (row - 1)), (cols - 1 - at, at - (cols - 5 + row))):
        cell = jnp.where((first == 0) & (row >= 1) & (row <= 4), F32(1.0), F32(0.0))
        cell = jnp.where(row == 0, powers_of(smooth.ratio, place, 7), cell)
        parts.append(jnp.where(row == 5, powers_of(deriv.ratio, place, 7), cell))
    hi, lo = split(jnp.concatenate(parts, axis=0))
    return jnp.concatenate(
        [jnp.concatenate([hi, hi], axis=1), jnp.concatenate([lo, jnp.zeros_like(lo)], axis=1)], axis=0
    )


def geometric(values, ratio, weights, tail):
    tiles = [values[8 * j : 8 * j + 8] for j in range(values.shape[0] // 8)]
    if not tail:
        tiles = tiles[::-1]
    total = tiles[0]
    for tile in tiles[1:]:
        total = total * F32(ratio**8) + tile
    return jnp.sum(total * weights, axis=0, keepdims=True)


def face_kernel(f_hbm, f, y_down, y_up, sems):
    cols = f.shape[2]
    reads = []
    for i, (first, planes) in enumerate(pieces):
        part = pl.ds(first, planes)
        reads.append(pltpu.make_async_copy(f_hbm.at[part], f.at[part], sems.at[i]))
        reads[-1].start()
    ty = y_functionals(cols)
    for read, (first, planes) in zip(reads, pieces):
        read.wait()
        for p in range(first, first + planes):
            both = jnp.concatenate(split(f[p]), axis=-1)
            r = dot(ty, both, ((1,), (1,)))
            r = r[:16] + r[16:]
            for k in range(6):
                y_down[k, p : p + 1, :] = r[k : k + 1]
                y_up[k, p : p + 1, :] = r[8 + k : 9 + k]


def windows(cells, margin):
    pieces, first = [], 0
    while first < cells:
        start = min(max(0, (first - margin) // 16 * 16), cells - 128)
        end = cells if start == cells - 128 else (start + 128 - margin) // 8 * 8
        pieces.append((first, end - first, start))
        first = end
    return pieces


def window_weights(line, cells, margin):
    block = line.block(cells)
    tables = []
    for first, count, start in windows(cells, margin):
        hi, lo = halves(block[first : first + count, start : start + 128])
        tables.append(np.block([[hi, hi], [lo, np.zeros_like(lo)]]))
    return np.concatenate(tables, axis=0)


def x_operator(hi, lo, w, margin):
    parts = []
    for first, count, start in windows(hi.shape[0], margin):
        cells = jnp.concatenate([hi[start : start + 128], lo[start : start + 128]], axis=0)
        r = dot(w[2 * first : 2 * (first + count)], cells)
        parts.append(r[:count] + r[count:])
    r = jnp.concatenate(parts, axis=0)
    return r[:, :128], r[:, 128:]


def sweep(planes, body, written, size=chunk):
    started = []
    for p in range(0, planes, 2):
        body(p)
        if (p + 2) % size == 0:
            copies = written(p + 2 - size, size)
            for copy in copies:
                copy.start()
            started += copies
    for copy in started:
        copy.wait()


def dot3(rows, table):
    n = table.shape[1] // 2
    a, b = split(rows)
    r = dot(a, table[...])
    return r[:, :n] + r[:, n:] + dot(b, table[:, :n])


def local_kernel(f, wx, wy, by, dx_out, part_y, dx_low, dx_high, down, up, own, dx, sems):
    planes, n, cols = f.shape
    deriv, smooth = line_operators()
    at = lax.broadcasted_iota(jnp.int32, (8, cols), 0)
    d_head, d_tail = powers_of(deriv.ratio, at, 3), powers_of(deriv.ratio, 7 - at, 3)
    f_head, f_tail = powers_of(smooth.ratio, at, 3), powers_of(smooth.ratio, 7 - at, 3)
    inner = pl.ds(deriv_rim, n - 2 * deriv_rim)

    def written(first, count):
        part = pl.ds(first, count)
        return [pltpu.make_async_copy(dx.at[part, inner], dx_out.at[part, inner], sems.at[first // chunk])]

    def body(p):
        hi, lo = split(jnp.concatenate([f[p], f[p + 1]], axis=-1))
        for j in range(2):
            at = slice(cols * j, cols * j + cols)
            part_y[p + j] = dot(jnp.concatenate([hi[:, at], lo[:, at]], axis=-1), wy[...])
        for j, r in enumerate(x_operator(hi, lo, wx, deriv_rim)):
            q = p + j
            dx[q] = r
            dx_low[q] = r[:deriv_rim]
            dx_high[q] = r[n - deriv_rim :]
            row = slice(q, q + 1)
            down[0, row, :] = geometric(f[q, :reach, :], smooth.ratio, f_head, False)
            up[0, row, :] = geometric(f[q, n - reach :, :], smooth.ratio, f_tail, True)
            down[5, row, :] = geometric(f[q, : reach // 2, :], deriv.ratio, d_head, False)
            up[5, row, :] = geometric(f[q, n - reach // 2 :, :], deriv.ratio, d_tail, True)
            for k in range(4):
                down[1 + k, row, :] = f[q, k : k + 1, :]
                up[1 + k, row, :] = f[q, n - 4 + k : n - 3 + k, :]

    sweep(planes, body, written)
    rows = jnp.concatenate([down[k] for k in range(5)] + [up[k] for k in range(5)], axis=0)
    own[...] = dot3(rows, by[...])


def x_face_kernel(own, x_down, x_up, lower, upper, tx, vy, down, up):
    planes = lower.shape[1]
    rows = jnp.concatenate([lower[g] for g in range(5)] + [upper[g] for g in range(5)], axis=0)
    r = dot3(rows, tx[...])
    z = r[:planes]
    for g in range(1, 10):
        z = z + pltpu.roll(r[g * planes : (g + 1) * planes], 10 * g, 1)
    rows = jnp.concatenate([z] + [pltpu.roll(z, 128 - k, 1) for k in range(1, 10)], axis=0)
    total = own[...] + dot3(rows, vy[...])
    for k in range(5):
        down[k] = total[k * planes : (k + 1) * planes]
        up[k] = total[(5 + k) * planes : (6 + k) * planes]
    down[5] = x_down[5]
    up[5] = x_up[5]
    down[6] = x_down[1]
    up[6] = x_up[4]


def late_kernel(f, part_y, lower, upper, wy, wx, dy_out, sm_out, sm_low, sm_high, halo, dy, gy, sm, sems):
    planes, n, cols = f.shape
    zero = jnp.zeros((planes, 128), F32)
    for c in range(0, n, 128):
        for k in range(16):
            rows = lower[k, :, c : c + 128] if k < 6 else upper[k - 6, :, c : c + 128] if k < 12 else zero
            halo[c // 128, pl.ds(k, planes, stride=16), :] = rows
    inner = pl.ds(filter_rim, n - 2 * filter_rim)

    started = []

    def send(source, target, number):
        started.append(pltpu.make_async_copy(source, target, number))
        started[-1].start()

    def y_rows(p):
        for q in (p, p + 1):
            at = slice(16 * q, 16 * q + 16)
            hi, lo = split(jnp.concatenate([halo[c, at, :] for c in range(n // 128)], axis=-1))
            faces = jnp.concatenate([hi, lo, hi], axis=0).T
            r = dot(jnp.concatenate([f[q].astype(BF16), faces], axis=-1), wy[...]) + part_y[q]
            dy[q] = r[:, :cols]
            gy[q] = r[:, cols:]

    def x_rows(p):
        hi, lo = split(jnp.concatenate([gy[p], gy[p + 1]], axis=-1))
        for j, r in enumerate(x_operator(hi, lo, wx, filter_rim)):
            sm[p + j] = r
            sm_low[p + j] = r[:filter_rim]
            sm_high[p + j] = r[n - filter_rim :]

    for p in range(0, planes + lag, 2):
        if p < planes:
            y_rows(p)
        if p >= lag:
            x_rows(p - lag)
        if p < planes and (p + 2) % chunk == 0:
            part = pl.ds(p + 2 - chunk, chunk)
            send(dy.at[part], dy_out.at[part], sems.at[0, p // chunk])
        if p >= lag and (p - lag + 2) % chunk == 0:
            part = pl.ds(p - lag + 2 - chunk, chunk)
            send(sm.at[part, inner], sm_out.at[part, inner], sems.at[1, (p - lag) // chunk])
    for copy in started:
        copy.wait()


def rim_kernel(
    dx_low, dx_high, sm_low, sm_high, lower, upper, ds_low, ds_high, dc_low, dc_high, fs_low, fs_high, fc_low, fc_high,
    dx_in, sm_in, dx_out, sm_out, dl, dh, sl, sh, sems,
):
    planes = dx_low.shape[0]
    n = dx_out.shape[1]

    def written(first, count):
        part, number = pl.ds(first, count), first // rim_chunk
        return [
            pltpu.make_async_copy(sl.at[part], sm_out.at[part, pl.ds(0, filter_rim)], sems.at[0, number]),
            pltpu.make_async_copy(sh.at[part], sm_out.at[part, pl.ds(n - filter_rim, filter_rim)], sems.at[1, number]),
            pltpu.make_async_copy(dl.at[part], dx_out.at[part, pl.ds(0, deriv_rim)], sems.at[2, number]),
            pltpu.make_async_copy(dh.at[part], dx_out.at[part, pl.ds(n - deriv_rim, deriv_rim)], sems.at[3, number]),
        ]

    def body(q):
        for p in (q, q + 1):
            row = slice(p, p + 1)
            low = dx_low[p] + ds_low[...] * lower[5, row, :]
            high = dx_high[p] + ds_high[...] * upper[5, row, :]
            dl[p] = jnp.concatenate([low[:8] + dc_low[...] * lower[6, row, :], low[8:]], axis=0)
            dh[p] = jnp.concatenate([high[:-8], high[-8:] + dc_high[...] * upper[6, row, :]], axis=0)
            low = sm_low[p] + fs_low[...] * lower[0, row, :]
            high = sm_high[p] + fs_high[...] * upper[0, row, :]
            near_low, near_high = low[:8], high[-8:]
            for k in range(4):
                near_low = near_low + fc_low[k] * lower[1 + k, row, :]
                near_high = near_high + fc_high[k] * upper[1 + k, row, :]
            sl[p] = jnp.concatenate([near_low, low[8:]], axis=0)
            sh[p] = jnp.concatenate([high[:-8], near_high], axis=0)

    sweep(planes, body, written, rim_chunk)


def tables(rows, cols):
    deriv, smooth = line_operators()
    t = {"wx_d": window_weights(deriv, rows, deriv_rim), "wx_f": window_weights(smooth, rows, filter_rim)}
    d_hi, d_lo = halves(deriv.block(cols).T)
    f_hi, f_lo = halves(smooth.block(cols).T)
    hi, lo = np.concatenate([d_hi, f_hi], axis=1), np.concatenate([d_lo, f_lo], axis=1)
    v = np.zeros((16, 2 * cols))
    low, high = smooth.from_below(cols), smooth.from_above(cols)
    v[0:5, cols:], v[6:11, cols:] = low.T, high.T
    low, high = deriv.from_below(cols), deriv.from_above(cols)
    v[5, :cols], v[4, :cols] = low[:, 0], low[:, 4]
    v[11, :cols], v[7, :cols] = high[:, 0], high[:, 1]
    v_hi, v_lo = halves(v)
    t["wy"] = np.concatenate([hi, hi], axis=0)
    t["wy_more"] = np.concatenate([lo, v_hi, v_hi, v_lo], axis=0)
    powers = lambda line, count: line.ratio ** np.arange(count)
    hi, lo = halves(smooth.block(cols).T)
    t["by"] = np.concatenate([hi, lo], axis=1)
    tx = np.zeros((rows, 128))
    tx[:, 0] = powers(smooth, rows)
    tx[:, 5] = tx[::-1, 0]
    for k in range(4):
        tx[k, 1 + k] = 1.0
        tx[rows - 4 + k, 6 + k] = 1.0
    hi, lo = halves(tx)
    t["tx"] = np.concatenate([hi, lo], axis=1)
    low, high = smooth.from_below(cols), smooth.from_above(cols)
    vy = np.zeros((128, cols))
    for g in range(5):
        vy[10 * g] = low[:, g]
        vy[10 * (5 + g)] = high[:, g]
    hi, lo = halves(vy)
    t["vy"] = np.concatenate([hi, lo], axis=1)
    low, high = smooth.from_below(rows), smooth.from_above(rows)
    t["fs_low"], t["fs_high"] = lanes(low[:filter_rim, 0]), lanes(high[-filter_rim:, 0])
    t["fc_low"] = np.stack([lanes(low[:8, 1 + k]) for k in range(4)])
    t["fc_high"] = np.stack([lanes(high[-8:, 1 + k]) for k in range(4)])
    low, high = deriv.from_below(rows), deriv.from_above(rows)
    t["ds_low"], t["ds_high"] = lanes(low[:deriv_rim, 0]), lanes(high[-deriv_rim:, 0])
    t["dc_low"], t["dc_high"] = lanes(low[:8, 4]), lanes(high[-8:, 1])
    return {key: jnp.asarray(value) for key, value in t.items()}


def shifted(values, axis, by):
    count = lax.axis_size(axis)
    return lax.ppermute(values, axis, [(i, (i + by) % count) for i in range(count)])


def on_device(fields):
    shape = fields.shape
    rows, cols = shape[2:]
    planes = shape[0] * shape[1]
    block = (planes, rows, cols)
    t = tables(rows, cols)
    y_face = (6, planes, rows)
    dx_rim, sm_rim = (planes, deriv_rim, cols), (planes, filter_rim, cols)
    f, y_down, y_up = call(
        "faces", face_kernel, [block, y_face, y_face],
        [pltpu.with_memory_space_constraint(fields.reshape(block), pltpu.HBM)], 10**9, 10**7,
        in_specs=[ANY], scratch=[pltpu.SemaphoreType.DMA((len(pieces),))],
    )
    y_lower = shifted(y_up, "gy", 1)
    y_upper = shifted(y_down, "gy", -1)
    face = (7, planes, cols)
    copies = planes // chunk
    dx, part_y, dx_low, dx_high, x_down, x_up, own = call(
        "local", local_kernel,
        [block, (planes, rows, 2 * cols), dx_rim, dx_rim, (6, planes, cols), (6, planes, cols), (10 * planes, cols)],
        [f, t["wx_d"], t["wy"], t["by"]], 4 * 10**9, 10**7,
        out_specs=[ANY] + [VMEM] * 6, scratch=[pltpu.VMEM(block, F32), pltpu.SemaphoreType.DMA((copies,))],
    )
    x_down, x_up = call(
        "x_faces", x_face_kernel, [face, face], [own, x_down, x_up, y_lower, y_upper, t["tx"], t["vy"]], 10**8, 10**6
    )
    x_lower = shifted(x_up, "gx", 1)
    x_upper = shifted(x_down, "gx", -1)
    dy, sm, sm_low, sm_high = call(
        "late", late_kernel, [block, block, sm_rim, sm_rim],
        [f, part_y, y_lower, y_upper, t["wy_more"], t["wx_f"]], 6 * 10**9, 2 * 10**7,
        out_specs=[ANY, ANY, VMEM, VMEM],
        scratch=[
            pltpu.VMEM((rows // 128, planes * 16, 128), F32),
            pltpu.VMEM(block, F32),
            pltpu.VMEM(block, F32),
            pltpu.VMEM(block, F32),
            pltpu.SemaphoreType.DMA((2, copies)),
        ],
        limit=24,
    )
    rims = ("ds_low", "ds_high", "dc_low", "dc_high", "fs_low", "fs_high", "fc_low", "fc_high")
    ins = [dx_low, dx_high, sm_low, sm_high, x_lower, x_upper] + [t[k] for k in rims]
    dx, sm = call(
        "rims", rim_kernel, [block, block], ins + [dx, sm], 10**8, 4 * 10**6,
        in_specs=[VMEM] * len(ins) + [ANY, ANY],
        out_specs=[ANY, ANY],
        scratch=[pltpu.VMEM(shape, F32) for shape in (dx_rim, dx_rim, sm_rim, sm_rim)]
        + [pltpu.SemaphoreType.DMA((4, planes // rim_chunk))],
        aliases={len(ins): 0, len(ins) + 1: 1},
    )
    return tuple(out.reshape(shape) for out in (dx, dy, sm))


def solution(mesh):
    placed = P(None, None, "gx", "gy")
    return jax.shard_map(
        on_device, mesh=mesh, in_specs=(placed,), out_specs=(placed, placed, placed), check_vma=False
    )
```

```python
import math

import jax
import jax.numpy as jnp
import ml_dtypes
import numpy as np
from jax import lax
from jax.experimental import pallas as pl
from jax.experimental.pallas import tpu as pltpu
from jax.sharding import PartitionSpec as P

F32 = jnp.float32
BF16 = jnp.bfloat16
deriv_offdiag = 1.0 / 3.0
coef_near = 14.0 / 9.0
coef_far = 1.0 / 9.0
filter_offdiag = 0.45
reach = 64
filter_rim = 40
deriv_rim = 24
pieces = ((0, 8), (8, 8), (16, 8), (24, 8), (32, 8))
chunk = 4
lag = 8
ahead = 16
rim_chunk = 8


def filter_weights():
    return [
        (193.0 + 126.0 * filter_offdiag) / 256.0,
        (105.0 + 302.0 * filter_offdiag) / 256.0,
        15.0 * (2.0 * filter_offdiag - 1.0) / 64.0,
        45.0 * (1.0 - 2.0 * filter_offdiag) / 512.0,
        5.0 * (2.0 * filter_offdiag - 1.0) / 256.0,
        (1.0 - 2.0 * filter_offdiag) / 512.0,
    ]


class Line:
    def __init__(self, offdiag, taps, sign, width):
        gap = math.sqrt(1.0 - 4.0 * offdiag * offdiag)
        self.ratio = (gap - 1.0) / (2.0 * offdiag)
        self.gap = gap
        self.taps = taps
        self.sign = sign
        far = width + 4
        self.scale = self.tap(far) / self.ratio**far
        self.near = [0.0] + [
            self.tap(n) - self.scale * self.ratio**n if n <= width else 0.0 for n in range(1, 2 * far)
        ]

    def tap(self, n):
        return sum(w * self.ratio ** abs(n - o) / self.gap for o, w in self.taps)

    def block(self, cells):
        values = np.array([self.tap(n) for n in range(-cells + 1, cells)])
        ids = np.arange(cells)
        return values[ids[None, :] - ids[:, None] + cells - 1]

    def near_at(self, n):
        return self.near[n] if 0 < n < len(self.near) else 0.0

    def from_below(self, cells):
        table = np.zeros((cells, 5))
        for i in range(cells):
            table[i, 0] = self.sign * self.scale * self.ratio ** (i + 1)
            for k in range(4):
                table[i, 1 + k] = self.sign * self.near_at(i + 4 - k)
        return table

    def from_above(self, cells):
        table = np.zeros((cells, 5))
        for i in range(cells):
            table[i, 0] = self.scale * self.ratio ** (cells - i)
            for k in range(4):
                table[i, 1 + k] = self.near_at(cells + k - i)
        return table


def line_operators():
    weights = filter_weights()
    deriv_taps = [
        (-2, -coef_far / 4.0),
        (-1, -coef_near / 2.0),
        (1, coef_near / 2.0),
        (2, coef_far / 4.0),
    ]
    filter_taps = [(0, weights[0])]
    for order in range(1, 6):
        filter_taps.append((order, weights[order] / 2.0))
        filter_taps.append((-order, weights[order] / 2.0))
    return Line(deriv_offdiag, deriv_taps, -1.0, 1), Line(filter_offdiag, filter_taps, 1.0, 4)


def halves(table):
    hi = np.asarray(table, np.float32).astype(ml_dtypes.bfloat16)
    lo = (np.asarray(table, np.float64) - hi.astype(np.float64)).astype(ml_dtypes.bfloat16)
    return hi, lo


def split(values):
    hi = values.astype(BF16)
    return hi, (values - hi.astype(F32)).astype(BF16)


def dot(a, b, dims=((1,), (0,))):
    return lax.dot_general(a, b, (dims, ((), ())), preferred_element_type=F32)


def lanes(column):
    return np.repeat(np.asarray(column, np.float32)[:, None], 128, axis=1)


VMEM = pl.BlockSpec(memory_space=pltpu.VMEM)
ANY = pl.BlockSpec(memory_space=pl.ANY)


def call(name, kernel, outs, ins, flops, nbytes, in_specs=None, out_specs=None, scratch=(), limit=20, aliases=None):
    return pl.pallas_call(
        kernel,
        in_specs=in_specs or [VMEM] * len(ins),
        out_specs=out_specs or [VMEM] * len(outs),
        out_shape=[jax.ShapeDtypeStruct(shape, F32) for shape in outs],
        scratch_shapes=list(scratch),
        input_output_aliases=aliases or {},
        compiler_params=pltpu.CompilerParams(vmem_limit_bytes=limit << 20),
        cost_estimate=pl.CostEstimate(flops=flops, bytes_accessed=nbytes, transcendentals=0),
        name=name,
    )(*ins)


def powers_of(ratio, exponent, bits):
    out = jnp.where(exponent & 1 == 1, F32(ratio), F32(1.0))
    for b in range(1, bits):
        out = out * jnp.where((exponent >> b) & 1 == 1, F32(ratio ** (1 << b)), F32(1.0))
    return out


def y_functionals(cols):
    deriv, smooth = line_operators()
    shape = (8, cols)
    at = lax.broadcasted_iota(jnp.int32, shape, 1)
    row = lax.broadcasted_iota(jnp.int32, shape, 0)
    parts = []
    for place, first in ((at, at - (row - 1)), (cols - 1 - at, at - (cols - 5 + row))):
        cell = jnp.where((first == 0) & (row >= 1) & (row <= 4), F32(1.0), F32(0.0))
        cell = jnp.where(row == 0, powers_of(smooth.ratio, place, 7), cell)
        parts.append(jnp.where(row == 5, powers_of(deriv.ratio, place, 7), cell))
    hi, lo = split(jnp.concatenate(parts, axis=0))
    return jnp.concatenate(
        [jnp.concatenate([hi, hi], axis=1), jnp.concatenate([lo, jnp.zeros_like(lo)], axis=1)], axis=0
    )


def geometric(values, ratio, weights, tail):
    tiles = [values[8 * j : 8 * j + 8] for j in range(values.shape[0] // 8)]
    if not tail:
        tiles = tiles[::-1]
    total = tiles[0]
    for tile in tiles[1:]:
        total = total * F32(ratio**8) + tile
    return jnp.sum(total * weights, axis=0, keepdims=True)


def face_kernel(f_hbm, f, y_down, y_up, sems):
    cols = f.shape[2]
    reads = []
    for i, (first, planes) in enumerate(pieces):
        part = pl.ds(first, planes)
        reads.append(pltpu.make_async_copy(f_hbm.at[part], f.at[part], sems.at[i]))
        reads[-1].start()
    ty = y_functionals(cols)
    for read, (first, planes) in zip(reads, pieces):
        read.wait()
        for p in range(first, first + planes):
            both = jnp.concatenate(split(f[p]), axis=-1)
            r = dot(ty, both, ((1,), (1,)))
            r = r[:16] + r[16:]
            for k in range(6):
                y_down[k, p : p + 1, :] = r[k : k + 1]
                y_up[k, p : p + 1, :] = r[8 + k : 9 + k]


def windows(cells, margin):
    pieces, first = [], 0
    while first < cells:
        start = min(max(0, (first - margin) // 16 * 16), cells - 128)
        end = cells if start == cells - 128 else (start + 128 - margin) // 8 * 8
        pieces.append((first, end - first, start))
        first = end
    return pieces


def window_weights(line, cells, margin):
    block = line.block(cells)
    tables = []
    for first, count, start in windows(cells, margin):
        hi, lo = halves(block[first : first + count, start : start + 128])
        tables.append(np.block([[hi, hi], [lo, np.zeros_like(lo)]]))
    return np.concatenate(tables, axis=0)


def x_operator(hi, lo, w, margin):
    parts = []
    for first, count, start in windows(hi.shape[0], margin):
        cells = jnp.concatenate([hi[start : start + 128], lo[start : start + 128]], axis=0)
        r = dot(w[2 * first : 2 * (first + count)], cells)
        parts.append(r[:count] + r[count:])
    r = jnp.concatenate(parts, axis=0)
    return r[:, :128], r[:, 128:]


def sweep(planes, body, written, size=chunk):
    started = []
    for p in range(0, planes, 2):
        body(p)
        if (p + 2) % size == 0:
            copies = written(p + 2 - size, size)
            for copy in copies:
                copy.start()
            started += copies
    for copy in started:
        copy.wait()


def dot3(rows, table):
    n = table.shape[1] // 2
    a, b = split(rows)
    r = dot(a, table[...])
    return r[:, :n] + r[:, n:] + dot(b, table[:, :n])


def local_kernel(f, wx, wy, wy_more, wx_f, by, dx_out, part_y, dx_low, dx_high, down, up, own, dx, sems):
    planes, n, cols = f.shape
    deriv, smooth = line_operators()
    at = lax.broadcasted_iota(jnp.int32, (8, cols), 0)
    d_head, d_tail = powers_of(deriv.ratio, at, 3), powers_of(deriv.ratio, 7 - at, 3)
    f_head, f_tail = powers_of(smooth.ratio, at, 3), powers_of(smooth.ratio, 7 - at, 3)
    inner = pl.ds(deriv_rim, n - 2 * deriv_rim)

    def written(first, count):
        part = pl.ds(first, count)
        return [pltpu.make_async_copy(dx.at[part, inner], dx_out.at[part, inner], sems.at[first // chunk])]

    def body(p):
        hi, lo = split(jnp.concatenate([f[p], f[p + 1]], axis=-1))
        for j in range(2):
            at = slice(cols * j, cols * j + cols)
            if p < ahead:
                weights = jnp.concatenate([wy[...], wy_more[:cols]], axis=0)
                part_y[p + j] = dot(jnp.concatenate([hi[:, at], lo[:, at], hi[:, at]], axis=-1), weights)
            else:
                part_y[p + j] = dot(jnp.concatenate([hi[:, at], lo[:, at]], axis=-1), wy[...])
        for j, r in enumerate(x_operator(hi, lo, wx, deriv_rim)):
            q = p + j
            dx[q] = r
            dx_low[q] = r[:deriv_rim]
            dx_high[q] = r[n - deriv_rim :]
            row = slice(q, q + 1)
            down[0, row, :] = geometric(f[q, :reach, :], smooth.ratio, f_head, False)
            up[0, row, :] = geometric(f[q, n - reach :, :], smooth.ratio, f_tail, True)
            down[5, row, :] = geometric(f[q, : reach // 2, :], deriv.ratio, d_head, False)
            up[5, row, :] = geometric(f[q, n - reach // 2 :, :], deriv.ratio, d_tail, True)
            for k in range(4):
                down[1 + k, row, :] = f[q, k : k + 1, :]
                up[1 + k, row, :] = f[q, n - 4 + k : n - 3 + k, :]

        if lag <= p < ahead + lag:
            hi, lo = split(jnp.concatenate([part_y[p - lag, :, cols:], part_y[p - lag + 1, :, cols:]], axis=-1))
            for j, r in enumerate(x_operator(hi, lo, wx_f, filter_rim)):
                part_y[p - lag + j, :, cols:] = r

    sweep(planes, body, written)
    rows = jnp.concatenate([down[k] for k in range(5)] + [up[k] for k in range(5)], axis=0)
    own[...] = dot3(rows, by[...])


def x_face_kernel(own, x_down, x_up, lower, upper, tx, vy, down, up):
    planes = lower.shape[1]
    rows = jnp.concatenate([lower[g] for g in range(5)] + [upper[g] for g in range(5)], axis=0)
    r = dot3(rows, tx[...])
    z = r[:planes]
    for g in range(1, 10):
        z = z + pltpu.roll(r[g * planes : (g + 1) * planes], 10 * g, 1)
    rows = jnp.concatenate([z] + [pltpu.roll(z, 128 - k, 1) for k in range(1, 10)], axis=0)
    total = own[...] + dot3(rows, vy[...])
    for k in range(5):
        down[k] = total[k * planes : (k + 1) * planes]
        up[k] = total[(5 + k) * planes : (6 + k) * planes]
    down[5] = x_down[5]
    up[5] = x_up[5]
    down[6] = x_down[1]
    up[6] = x_up[4]


def late_kernel(f, part_y, lower, upper, wy, wx, wy_ahead, ax, dy_out, sm_out, sm_low, sm_high, halo, dy, gy, sm, sems):
    planes, n, cols = f.shape
    rows = jnp.concatenate([h[k, :ahead, :] for h in (lower, upper) for k in range(5)], axis=0)
    done = dot3(rows, ax[...])
    table = []
    for h, first in ((lower, 0), (upper, 5)):
        for k in range(5):
            at = (first + k) * ahead
            table.append(jnp.concatenate([done[at : at + ahead], h[k, ahead:, :]], axis=0))
        table.append(h[5])
    table += [lower[4], upper[1]]
    zero = jnp.zeros((planes, 128), F32)
    for c in range(0, n, 128):
        for k in range(16):
            halo[c // 128, pl.ds(k, planes, stride=16), :] = table[k][:, c : c + 128] if k < len(table) else zero
    inner = pl.ds(filter_rim, n - 2 * filter_rim)

    started = []

    def send(source, target, number):
        started.append(pltpu.make_async_copy(source, target, number))
        started[-1].start()

    def faces(q):
        at = slice(16 * q, 16 * q + 16)
        hi, lo = split(jnp.concatenate([halo[c, at, :] for c in range(n // 128)], axis=-1))
        return jnp.concatenate([hi, lo, hi], axis=0).T

    def keep(q, r):
        sm[q] = r
        sm_low[q] = r[:filter_rim]
        sm_high[q] = r[n - filter_rim :]

    def y_rows(p):
        for q in (p, p + 1):
            if q < ahead:
                r = dot(faces(q), wy_ahead[...]) + part_y[q]
                keep(q, r[:, cols:])
            else:
                r = dot(jnp.concatenate([f[q].astype(BF16), faces(q)], axis=-1), wy[...]) + part_y[q]
                gy[q] = r[:, cols:]
            dy[q] = r[:, :cols]

    def x_rows(p):
        hi, lo = split(jnp.concatenate([gy[p], gy[p + 1]], axis=-1))
        for j, r in enumerate(x_operator(hi, lo, wx, filter_rim)):
            keep(p + j, r)

    def send_filtered(p):
        if (p + 2) % chunk == 0:
            part = pl.ds(p + 2 - chunk, chunk)
            send(sm.at[part, inner], sm_out.at[part, inner], sems.at[1, p // chunk])

    for p in range(0, planes + lag, 2):
        if p < planes:
            y_rows(p)
            if (p + 2) % chunk == 0:
                part = pl.ds(p + 2 - chunk, chunk)
                send(dy.at[part], dy_out.at[part], sems.at[0, p // chunk])
            if p < ahead:
                send_filtered(p)
        if p >= ahead + lag:
            x_rows(p - lag)
            send_filtered(p - lag)
    for copy in started:
        copy.wait()


def rim_kernel(
    dx_low, dx_high, sm_low, sm_high, lower, upper, ds_low, ds_high, dc_low, dc_high, fs_low, fs_high, fc_low, fc_high,
    dx_in, sm_in, dx_out, sm_out, dl, dh, sl, sh, sems,
):
    planes = dx_low.shape[0]
    n = dx_out.shape[1]

    def written(first, count):
        part, number = pl.ds(first, count), first // rim_chunk
        return [
            pltpu.make_async_copy(sl.at[part], sm_out.at[part, pl.ds(0, filter_rim)], sems.at[0, number]),
            pltpu.make_async_copy(sh.at[part], sm_out.at[part, pl.ds(n - filter_rim, filter_rim)], sems.at[1, number]),
            pltpu.make_async_copy(dl.at[part], dx_out.at[part, pl.ds(0, deriv_rim)], sems.at[2, number]),
            pltpu.make_async_copy(dh.at[part], dx_out.at[part, pl.ds(n - deriv_rim, deriv_rim)], sems.at[3, number]),
        ]

    def body(q):
        for p in (q, q + 1):
            row = slice(p, p + 1)
            low = dx_low[p] + ds_low[...] * lower[5, row, :]
            high = dx_high[p] + ds_high[...] * upper[5, row, :]
            dl[p] = jnp.concatenate([low[:8] + dc_low[...] * lower[6, row, :], low[8:]], axis=0)
            dh[p] = jnp.concatenate([high[:-8], high[-8:] + dc_high[...] * upper[6, row, :]], axis=0)
            low = sm_low[p] + fs_low[...] * lower[0, row, :]
            high = sm_high[p] + fs_high[...] * upper[0, row, :]
            near_low, near_high = low[:8], high[-8:]
            for k in range(4):
                near_low = near_low + fc_low[k] * lower[1 + k, row, :]
                near_high = near_high + fc_high[k] * upper[1 + k, row, :]
            sl[p] = jnp.concatenate([near_low, low[8:]], axis=0)
            sh[p] = jnp.concatenate([high[:-8], near_high], axis=0)

    sweep(planes, body, written, rim_chunk)


def tables(rows, cols):
    deriv, smooth = line_operators()
    t = {"wx_d": window_weights(deriv, rows, deriv_rim), "wx_f": window_weights(smooth, rows, filter_rim)}
    d_hi, d_lo = halves(deriv.block(cols).T)
    f_hi, f_lo = halves(smooth.block(cols).T)
    hi, lo = np.concatenate([d_hi, f_hi], axis=1), np.concatenate([d_lo, f_lo], axis=1)
    v = np.zeros((16, 2 * cols))
    low, high = smooth.from_below(cols), smooth.from_above(cols)
    v[0:5, cols:], v[6:11, cols:] = low.T, high.T
    low, high = deriv.from_below(cols), deriv.from_above(cols)
    v[5, :cols], v[4, :cols] = low[:, 0], low[:, 4]
    v[11, :cols], v[7, :cols] = high[:, 0], high[:, 1]
    v_hi, v_lo = halves(v)
    ahead_v = v.copy()
    ahead_v[[4, 7], :cols] = 0.0
    ahead_v[[12, 13], :cols] = v[[4, 7], :cols]
    ahead_hi, ahead_lo = halves(ahead_v)
    t["wy_ahead"] = np.concatenate([ahead_hi, ahead_hi, ahead_lo], axis=0)
    t["ax"] = np.concatenate(halves(smooth.block(rows).T), axis=1)
    t["wy"] = np.concatenate([hi, hi], axis=0)
    t["wy_more"] = np.concatenate([lo, v_hi, v_hi, v_lo], axis=0)
    powers = lambda line, count: line.ratio ** np.arange(count)
    hi, lo = halves(smooth.block(cols).T)
    t["by"] = np.concatenate([hi, lo], axis=1)
    tx = np.zeros((rows, 128))
    tx[:, 0] = powers(smooth, rows)
    tx[:, 5] = tx[::-1, 0]
    for k in range(4):
        tx[k, 1 + k] = 1.0
        tx[rows - 4 + k, 6 + k] = 1.0
    hi, lo = halves(tx)
    t["tx"] = np.concatenate([hi, lo], axis=1)
    low, high = smooth.from_below(cols), smooth.from_above(cols)
    vy = np.zeros((128, cols))
    for g in range(5):
        vy[10 * g] = low[:, g]
        vy[10 * (5 + g)] = high[:, g]
    hi, lo = halves(vy)
    t["vy"] = np.concatenate([hi, lo], axis=1)
    low, high = smooth.from_below(rows), smooth.from_above(rows)
    t["fs_low"], t["fs_high"] = lanes(low[:filter_rim, 0]), lanes(high[-filter_rim:, 0])
    t["fc_low"] = np.stack([lanes(low[:8, 1 + k]) for k in range(4)])
    t["fc_high"] = np.stack([lanes(high[-8:, 1 + k]) for k in range(4)])
    low, high = deriv.from_below(rows), deriv.from_above(rows)
    t["ds_low"], t["ds_high"] = lanes(low[:deriv_rim, 0]), lanes(high[-deriv_rim:, 0])
    t["dc_low"], t["dc_high"] = lanes(low[:8, 4]), lanes(high[-8:, 1])
    return {key: jnp.asarray(value) for key, value in t.items()}


def shifted(values, axis, by):
    count = lax.axis_size(axis)
    return lax.ppermute(values, axis, [(i, (i + by) % count) for i in range(count)])


def on_device(fields):
    shape = fields.shape
    rows, cols = shape[2:]
    planes = shape[0] * shape[1]
    block = (planes, rows, cols)
    t = tables(rows, cols)
    y_face = (6, planes, rows)
    dx_rim, sm_rim = (planes, deriv_rim, cols), (planes, filter_rim, cols)
    f, y_down, y_up = call(
        "faces", face_kernel, [block, y_face, y_face],
        [pltpu.with_memory_space_constraint(fields.reshape(block), pltpu.HBM)], 10**9, 10**7,
        in_specs=[ANY], scratch=[pltpu.SemaphoreType.DMA((len(pieces),))],
    )
    y_lower = shifted(y_up, "gy", 1)
    y_upper = shifted(y_down, "gy", -1)
    face = (7, planes, cols)
    copies = planes // chunk
    dx, part_y, dx_low, dx_high, x_down, x_up, own = call(
        "local", local_kernel,
        [block, (planes, rows, 2 * cols), dx_rim, dx_rim, (6, planes, cols), (6, planes, cols), (10 * planes, cols)],
        [f] + [t[k] for k in ("wx_d", "wy", "wy_more", "wx_f", "by")], 4 * 10**9, 10**7,
        out_specs=[ANY] + [VMEM] * 6, scratch=[pltpu.VMEM(block, F32), pltpu.SemaphoreType.DMA((copies,))],
    )
    x_down, x_up = call(
        "x_faces", x_face_kernel, [face, face], [own, x_down, x_up, y_lower, y_upper, t["tx"], t["vy"]], 10**8, 10**6
    )
    x_lower = shifted(x_up, "gx", 1)
    x_upper = shifted(x_down, "gx", -1)
    dy, sm, sm_low, sm_high = call(
        "late", late_kernel, [block, block, sm_rim, sm_rim],
        [f, part_y, y_lower, y_upper] + [t[k] for k in ("wy_more", "wx_f", "wy_ahead", "ax")], 6 * 10**9, 2 * 10**7,
        out_specs=[ANY, ANY, VMEM, VMEM],
        scratch=[
            pltpu.VMEM((rows // 128, planes * 16, 128), F32),
            pltpu.VMEM(block, F32),
            pltpu.VMEM(block, F32),
            pltpu.VMEM(block, F32),
            pltpu.SemaphoreType.DMA((2, copies)),
        ],
        limit=24,
    )
    rims = ("ds_low", "ds_high", "dc_low", "dc_high", "fs_low", "fs_high", "fc_low", "fc_high")
    ins = [dx_low, dx_high, sm_low, sm_high, x_lower, x_upper] + [t[k] for k in rims]
    dx, sm = call(
        "rims", rim_kernel, [block, block], ins + [dx, sm], 10**8, 4 * 10**6,
        in_specs=[VMEM] * len(ins) + [ANY, ANY],
        out_specs=[ANY, ANY],
        scratch=[pltpu.VMEM(shape, F32) for shape in (dx_rim, dx_rim, sm_rim, sm_rim)]
        + [pltpu.SemaphoreType.DMA((4, planes // rim_chunk))],
        aliases={len(ins): 0, len(ins) + 1: 1},
    )
    return tuple(out.reshape(shape) for out in (dx, dy, sm))


def solution(mesh):
    placed = P(None, None, "gx", "gy")
    return jax.shard_map(
        on_device, mesh=mesh, in_specs=(placed,), out_specs=(placed, placed, placed), check_vma=False
    )
```
